32 devices in a mesh: ctx: 2 (over y), exp: 16 (over z, x, core).
Axes of the slice: x: 2, y: 2, z: 4, core: 2. Of those that a mesh axis runs over, the one named last changes fastest.
Arguments:
- queries: bfloat16 [256, 8192], P('ctx', 'exp'), may hold values from -6 to 6
- keys: bfloat16 [256, 512], P('ctx'), may hold values from -6 to 6
- values: bfloat16 [256, 512], P('ctx'), may hold values from -5 to 5
- residual: bfloat16 [256, 4096], P(('ctx', 'exp')), may hold values from -6 to 6
- out_weight: bfloat16 [8192, 4096], P('exp'), may hold values from -0.125 to 0.125
- norm_gain: float32 [4096], replicated, may hold values from 0.25 to 1.75
- expert_ids: int32 [256, 8], P(('ctx', 'exp')), may hold values from 0 to 15, all different within a row; in each aligned block of 8 rows (0 to 7, 8 to 15, ...) at most 8 rows name the same one
- expert_gates: float32 [256, 8], P(('ctx', 'exp')), may hold values from 0.05 to 0.35
- w_gate: bfloat16 [16, 4096, 1536], P('exp', None, 'ctx'), may hold values from -0.09375 to 0.09375
- w_up: bfloat16 [16, 4096, 1536], P('exp', None, 'ctx'), may hold values from -0.09375 to 0.09375
- w_down: bfloat16 [16, 1536, 4096], P('exp', None, 'ctx'), may hold values from -0.3125 to 0.3125
Outputs:
- mixed: bfloat16 [256, 4096], P(('ctx', 'exp'))
- experts_out: bfloat16 [256, 4096], P(('ctx', 'exp'))
The draws below stay inside these ranges and needn't reach their ends.
Inputs may be any that keep to these rules, and one draw needn't show every extreme that they name: `expert_ids`: in each aligned block of 8 rows (the rows of one device) no expert is named by more than 8 rows, a bound that some block reaches.
All inputs are finite; a program needn't handle non-finite values.
Results may differ from the reference program's by a relative error of at most 0.034.
Values may be sent and summed in bfloat16 or wider, within the bound.
A program may use at most 64 MiB of HBM per device.

```python
import math
import jax
import jax.numpy as jnp
import numpy as np
from jax import lax

D = 4096
QUERY_HEAD_COUNT = 64
KEY_VALUE_HEADS = 4
HEAD_WIDTH = 128
FF = 1536
TOPK = 8
SEQUENCE_TOKENS = 256
EXPERTS = 16
TOK_DEV = 8
SLOTS = 8


def draw_queries(key, part):
    random_seed_key = jax.random.fold_in(key, 1)
    filled_tensor = jnp.clip(jax.random.normal(random_seed_key, (SEQUENCE_TOKENS, QUERY_HEAD_COUNT * HEAD_WIDTH), jnp.float32), -4.0, 4.0)
    return filled_tensor.astype(jnp.bfloat16)


def draw_keys(key, part):
    random_seed_key = jax.random.fold_in(key, 2)
    filled_tensor = jnp.clip(jax.random.normal(random_seed_key, (SEQUENCE_TOKENS, KEY_VALUE_HEADS * HEAD_WIDTH), jnp.float32), -4.0, 4.0)
    return filled_tensor.astype(jnp.bfloat16)


def block_levels(rng, shape, pieces, smallest, high):
    level, own = 1.0, jax.random.fold_in(rng, 6)
    for position, shards_of in pieces:
        draws = jnp.exp(jax.random.uniform(jax.random.fold_in(own, position), (shards_of,), jnp.float32, smallest / len(pieces), high / len(pieces)))
        level = level * jnp.repeat(draws, shape[position] // shards_of).reshape([-1 if axis == position else 1 for axis in range(len(shape))])
    return level


def assign_block(stream_key, own, number, rows, amount, top, bound, skew):
    order = jax.random.permutation(stream_key, amount)
    heavy_load, usual = shares(amount, rows * top, bound, skew, True), shares(amount, rows * top, bound, skew, False)
    places = jnp.arange(amount)

    def named(tallies, rotation):
        used = int((tallies > 0).sum())
        fixed = max(1, used // 4)
        passed = fixed + (places - fixed + rotation * (used - fixed)) % max(1, amount - fixed)
        return jnp.zeros((amount,), jnp.int32).at[order[jnp.where(places < fixed, places, passed)]].set(jnp.asarray(tallies, jnp.int32))

    tallies = jnp.where(number % 4 == 0, named(heavy_load, number // 4), named(usual, number - number // 4 - 1))
    mixed = jax.random.permutation(jax.random.fold_in(own, 3), amount)
    donor, taker = mixed[0:amount // 2 * 2:2], mixed[1:amount // 2 * 2:2]
    margin = jnp.minimum(tallies[donor] - 1, bound - tallies[taker]) // 2
    margin = jnp.where((donor == order[0]) | (taker == order[0]) | (tallies[taker] == 0), 0, jnp.maximum(margin, 0))
    passed = jax.random.randint(jax.random.fold_in(own, 4), (amount // 2,), 0, 1 << 20) % (margin + 1)
    tallies = tallies.at[donor].add(-passed).at[taker].add(passed)
    members = jnp.searchsorted(jnp.cumsum(tallies), jnp.arange(rows * top), side="right").astype(jnp.int32)
    table = members.reshape(top, rows).T
    table = table[jax.random.permutation(jax.random.fold_in(own, 1), rows)]
    rotation = jax.random.randint(jax.random.fold_in(own, 2), (rows, 1), 0, top)
    return jnp.take_along_axis(table, (jnp.arange(top)[None, :] + rotation) % top, axis=1)


def shares(amount, total, limit, skew, full):
    weights = [(1 << 20) // math.isqrt(grade ** skew) + 1 for grade in range(1, amount + 1)]
    largest = limit if full else min(limit, max(-(-total // amount), total * weights[0] // sum(weights)))
    least = 1 if total - largest >= amount - 1 else 0
    given, rest = [largest] + [least] * (amount - 1), total - largest - least * (amount - 1)
    while rest > 0:
        movable = [i for i in range(1, amount) if given[i] < largest] or [i for i in range(1, amount) if given[i] < limit]
        mass, left = sum([weights[i] for i in movable]), rest
        for i in movable:
            more = min(limit - given[i], max(1, left * weights[i] // mass), rest)
            given[i] = given[i] + more
            rest = rest - more
    return np.array(given)


def centred(stream_key, shape, spread, bound, shards=(), kind=jnp.bfloat16):
    drawn = spread * jax.random.normal(stream_key, shape, jnp.float32)
    if shards:
        drawn = drawn * block_levels(stream_key, shape, shards, -0.22, 0.18)
    return jnp.clip(drawn, -bound, bound).astype(kind)


def setup_inputs(seed: int = 0) -> dict:
    key_of = jax.random.split(jax.random.key(seed), 12)
    queries = draw_queries(jax.random.fold_in(key_of[11], 71), 0)
    keys = draw_keys(jax.random.fold_in(key_of[11], 71), 0)
    values = centred(key_of[2], (SEQUENCE_TOKENS, KEY_VALUE_HEADS * HEAD_WIDTH), 1.0, 5.0, ((0, 2),))
    residual = centred(key_of[3], (SEQUENCE_TOKENS, D), 1.0, 6.0, ((0, 32),))
    out_weight = centred(key_of[4], (QUERY_HEAD_COUNT * HEAD_WIDTH, D), (QUERY_HEAD_COUNT * HEAD_WIDTH // 4) ** -0.5, 0.125, ((0, 16),))
    norm_gain = jnp.clip(1.0 + 0.15 * jax.random.normal(key_of[5], (D,), jnp.float32), 0.25, 1.75)
    expert_ids_keys = jax.random.split(jax.random.fold_in(key_of[6], 1), SEQUENCE_TOKENS // TOK_DEV)
    expert_ids_turns = jax.random.permutation(jax.random.fold_in(key_of[6], 3), SEQUENCE_TOKENS // TOK_DEV)
    expert_ids = jax.vmap(lambda own, number: assign_block(jax.random.fold_in(key_of[6], 2), own, number, TOK_DEV, EXPERTS, TOPK, SLOTS, 2))(expert_ids_keys, expert_ids_turns).reshape((SEQUENCE_TOKENS, TOPK))
    expert_gates = jnp.clip(0.05 + 0.29999999 * jax.random.uniform(key_of[7], (SEQUENCE_TOKENS, TOPK), jnp.float32) ** block_levels(key_of[7], (SEQUENCE_TOKENS, TOPK), ((0, 32),), -0.2, 0.2), 0.05, 0.35)
    w_gate = centred(key_of[8], (EXPERTS, D, FF), D ** -0.5, 0.09375, ((0, 16), (2, 2)))
    w_up = centred(key_of[9], (EXPERTS, D, FF), D ** -0.5, 0.09375, ((0, 16), (2, 2)))
    w_down = centred(key_of[10], (EXPERTS, FF, D), (FF // 4) ** -0.5, 0.3125, ((0, 16), (2, 2)))
    return dict(queries=queries, keys=keys, values=values, residual=residual, out_weight=out_weight, norm_gain=norm_gain, expert_ids=expert_ids, expert_gates=expert_gates, w_gate=w_gate, w_up=w_up, w_down=w_down)


def reference(queries, keys, values, residual, out_weight, norm_gain, expert_ids, expert_gates, w_gate, w_up, w_down):
    group_width = QUERY_HEAD_COUNT // KEY_VALUE_HEADS
    scale = 1.0 / HEAD_WIDTH ** 0.5
    positions = jnp.arange(SEQUENCE_TOKENS, dtype=jnp.int32)
    allowed = positions[None, :] <= positions[:, None]

    def one_head(head):
        key_value_head = head // group_width
        query_cols = lax.dynamic_slice_in_dim(queries, (head * HEAD_WIDTH).astype(jnp.int32), HEAD_WIDTH, 1)
        key_cols = lax.dynamic_slice_in_dim(keys, (key_value_head * HEAD_WIDTH).astype(jnp.int32), HEAD_WIDTH, 1)
        value_cols = lax.dynamic_slice_in_dim(values, (key_value_head * HEAD_WIDTH).astype(jnp.int32), HEAD_WIDTH, 1)
        scores = jnp.dot(query_cols, key_cols.T, preferred_element_type=jnp.float32) * scale
        scores = jnp.where(allowed, scores, jnp.float32(-1e+30))
        row_max = lax.optimization_barrier(jnp.max(scores, axis=1, keepdims=True))
        weights = jnp.where(allowed, jnp.exp(scores - row_max), jnp.float32(0.0))
        total = lax.optimization_barrier(jnp.sum(weights, axis=1, keepdims=True))
        numer = jnp.dot(weights.astype(jnp.bfloat16), value_cols, preferred_element_type=jnp.float32)
        return (numer / total).astype(jnp.bfloat16)
    heads_all = lax.map(one_head, jnp.arange(QUERY_HEAD_COUNT, dtype=jnp.int32))
    heads_out = jnp.transpose(heads_all, (1, 0, 2)).reshape(SEQUENCE_TOKENS, QUERY_HEAD_COUNT * HEAD_WIDTH)
    projected = jnp.dot(heads_out, out_weight, preferred_element_type=jnp.float32)
    mixed = (residual.astype(jnp.float32) + projected).astype(jnp.bfloat16)
    stream = mixed.astype(jnp.float32)
    mean_sq = lax.optimization_barrier(jnp.mean(stream * stream, axis=1, keepdims=True))
    normed = (stream * lax.rsqrt(mean_sq + 1e-06) * norm_gain[None, :]).astype(jnp.bfloat16)
    most_rows = SEQUENCE_TOKENS // TOK_DEV * SLOTS
    slot_index = jnp.arange(most_rows, dtype=jnp.int32)

    def expert_step(accum, expert):
        picked = expert_ids == expert
        chosen = jnp.any(picked, axis=1)
        token_weight = lax.optimization_barrier(jnp.sum(jnp.where(picked, expert_gates, jnp.float32(0.0)), axis=1))
        count = jnp.sum(chosen.astype(jnp.int32))
        rows = jnp.nonzero(chosen, size=most_rows, fill_value=0)[0].astype(jnp.int32)
        inputs = normed[rows]
        gate = jnp.dot(inputs, w_gate[expert], preferred_element_type=jnp.float32)
        upper = jnp.dot(inputs, w_up[expert], preferred_element_type=jnp.float32)
        hidden = (jax.nn.silu(gate) * upper).astype(jnp.bfloat16)
        output = jnp.dot(hidden, w_down[expert], preferred_element_type=jnp.float32).astype(jnp.bfloat16)
        factor = jnp.where(slot_index < count, token_weight[rows], jnp.float32(0.0))
        accum = accum.at[rows].add(output.astype(jnp.float32) * factor[:, None])
        return (accum, None)
    start_acc = jnp.zeros((SEQUENCE_TOKENS, D), jnp.float32)
    accum, _ = lax.scan(expert_step, start_acc, jnp.arange(EXPERTS, dtype=jnp.int32))
    return (mixed, accum.astype(jnp.bfloat16))
```

```python
import jax
import jax.numpy as jnp
from jax import lax
from jax.experimental import pallas as pl
from jax.experimental.pallas import tpu as pltpu
from jax.sharding import PartitionSpec as P

QUERY_HEAD_COUNT = 64
KEY_VALUE_HEADS = 4
HEAD_WIDTH = 128


neg_large = -1e30
eps_norm = 1e-06


def shifted(value, axis, by):
    size = lax.axis_size(axis)
    pairs = [(i, i + by) for i in range(size) if 0 <= i + by < size]
    return lax.ppermute(value, axis, pairs)


def slot_numbers(expert_ids):
    tok_rows, top_count = expert_ids.shape
    flat_ids = expert_ids.reshape(-1)
    owner_row = jnp.arange(tok_rows * top_count, dtype=jnp.int32) // top_count
    earlier = (flat_ids[:, None] == flat_ids[None, :]) & (owner_row[None, :] < owner_row[:, None])
    return jnp.sum(earlier.astype(jnp.int32), axis=1).reshape(tok_rows, top_count)


def route_hits(expert_ids, slot_ids, expert_count, capacity):
    expert_hit = (
        expert_ids[None, None, :, :]
        == jnp.arange(expert_count, dtype=jnp.int32)[:, None, None, None]
    )
    slot_hit = (
        slot_ids[None, None, :, :] == jnp.arange(capacity, dtype=jnp.int32)[None, :, None, None]
    )
    return expert_hit & slot_hit


def expert_hidden(rows_block, gate_local, up_local):
    gate = jnp.dot(rows_block, gate_local, preferred_element_type=jnp.float32)
    upper = jnp.dot(rows_block, up_local, preferred_element_type=jnp.float32)
    return (jax.nn.silu(gate) * upper).astype(jnp.bfloat16)


def on_device(
    queries,
    keys,
    values,
    residual,
    out_weight,
    norm_gain,
    expert_ids,
    expert_gates,
    w_gate,
    w_up,
    w_down,
):
    tok_query = queries.shape[0]
    device_share = queries.shape[1] // HEAD_WIDTH
    ctx_pos = lax.axis_index("ctx")
    key_value_head = lax.axis_index("exp") * device_share // (QUERY_HEAD_COUNT // KEY_VALUE_HEADS)
    own_keys = lax.dynamic_slice_in_dim(keys, key_value_head * HEAD_WIDTH, HEAD_WIDTH, 1)
    own_values = lax.dynamic_slice_in_dim(values, key_value_head * HEAD_WIDTH, HEAD_WIDTH, 1)
    own_block = jnp.stack([own_keys, own_values])
    query_heads = queries.reshape(tok_query, device_share, HEAD_WIDTH)
    query_start = ctx_pos * tok_query
    query_pos = query_start + jnp.arange(tok_query, dtype=jnp.int32)
    scale = 1.0 / HEAD_WIDTH**0.5
    start_state = (
        jnp.full((device_share, tok_query), neg_large, jnp.float32),
        jnp.zeros((device_share, tok_query), jnp.float32),
        jnp.zeros((device_share, tok_query, HEAD_WIDTH), jnp.float32),
    )

    def attend(state_now, kv_piece, key_start):

        def compute(current):
            running_max, running_sum, weighted = current
            key_pos = key_start + jnp.arange(kv_piece.shape[1], dtype=jnp.int32)
            allowed = key_pos[None, :] <= query_pos[:, None]
            scores = (
                jnp.einsum(
                    "qhd,kd->hqk", query_heads, kv_piece[0], preferred_element_type=jnp.float32
                )
                * scale
            )
            scores = jnp.where(allowed[None], scores, neg_large)
            new_max = jnp.maximum(running_max, jnp.max(scores, axis=2))
            weights_blk = jnp.where(allowed[None], jnp.exp(scores - new_max[:, :, None]), 0.0)
            shrink = jnp.exp(running_max - new_max)
            new_sum = running_sum * shrink + jnp.sum(weights_blk, axis=2)
            added = jnp.einsum(
                "hqk,kd->hqd",
                weights_blk.astype(jnp.bfloat16),
                kv_piece[1],
                preferred_element_type=jnp.float32,
            )
            return (new_max, new_sum, weighted * shrink[:, :, None] + added)

        def unchanged(current):
            return current

        useful = (key_start >= 0) & (key_start <= query_start + tok_query - 1)
        return lax.cond(useful, compute, unchanged, state_now)

    ctx_count = lax.axis_size("ctx")
    state_now = attend(start_state, own_block, query_start)

    def cycle_turn(cycle_step, carried):
        state_cur, moving = carried
        moving = shifted(moving, "ctx", 1)
        source = ctx_pos - cycle_step
        return (attend(state_cur, moving, source * tok_query), moving)

    state_now, _ = lax.fori_loop(1, ctx_count, cycle_turn, (state_now, own_block))
    running_max, running_sum, weighted = state_now
    heads_done = (weighted / running_sum[:, :, None]).astype(jnp.bfloat16)
    heads_done = jnp.transpose(heads_done, (1, 0, 2)).reshape(tok_query, device_share * HEAD_WIDTH)
    tok_rows, top_count = expert_ids.shape
    projected = lax.psum_scatter(
        jnp.dot(heads_done, out_weight, preferred_element_type=jnp.float32).astype(jnp.bfloat16),
        "exp",
        scatter_dimension=0,
        tiled=True,
    ).astype(jnp.float32)
    mixed = (residual.astype(jnp.float32) + projected).astype(jnp.bfloat16)
    stream = mixed.astype(jnp.float32)
    mean_sq = jnp.mean(stream * stream, axis=1, keepdims=True)
    normed = (stream * lax.rsqrt(mean_sq + eps_norm) * norm_gain[None, :]).astype(jnp.bfloat16)
    expert_count = lax.axis_size("exp")
    ctx_count = lax.axis_size("ctx")
    capacity = min(tok_rows, 2 * tok_rows * top_count // expert_count)
    slot_ids = slot_numbers(expert_ids)
    hits = route_hits(expert_ids, slot_ids, expert_count, capacity)
    send_table = jnp.any(hits, axis=3).astype(jnp.bfloat16)
    gate_local = w_gate[0]
    up_local = w_up[0]
    down_local = w_down[0]
    width = normed.shape[1]
    outgoing = jnp.einsum(
        "ecm,md->ecd", send_table, normed, preferred_element_type=jnp.float32
    ).astype(jnp.bfloat16)
    arrived = lax.all_to_all(outgoing, "exp", split_axis=0, concat_axis=0, tiled=True)
    local_rows = arrived.reshape(-1, width)
    hidden = expert_hidden(
        lax.all_gather(local_rows, "ctx", axis=0, tiled=True), gate_local, up_local
    )
    expert_result = jnp.dot(
        lax.all_gather(hidden, "ctx", axis=1, tiled=True),
        down_local,
        preferred_element_type=jnp.float32,
    ).astype(jnp.bfloat16)
    expert_result = expert_result.reshape(ctx_count, expert_count, capacity, down_local.shape[1])
    returned = lax.all_to_all(
        lax.all_to_all(expert_result, "ctx", split_axis=0, concat_axis=3, tiled=True),
        "exp",
        split_axis=1,
        concat_axis=0,
        tiled=True,
    )
    returned = returned.reshape(expert_count, capacity, width)
    mix_table = jnp.sum(jnp.where(hits, expert_gates[None, None, :, :], 0.0), axis=3)
    experts_out = jnp.einsum(
        "ecm,ecd->md", mix_table, returned.astype(jnp.float32), precision=lax.Precision.HIGHEST
    )
    return (mixed, experts_out.astype(jnp.bfloat16))


BF = jnp.bfloat16
F32 = jnp.float32
ROWS = 16
EXTRA = 128
PROJ_PARTS = 4
FF_PARTS = 3
OUT_PARTS = 2


def layer_kernel(
    queries,
    keys,
    values,
    residual,
    norm_gain,
    expert_ids,
    expert_gates,
    wo_hbm,
    wg_hbm,
    wu_hbm,
    wd_hbm,
    mixed_out,
    experts_out,
    wo,
    wg,
    wu,
    wd,
    kv,
    res,
    table,
    heads,
    pc_send,
    pc_recv,
    px_send,
    px_recv,
    pz_send,
    pz_recv,
    proj,
    mixed_rows,
    rows_all,
    hidden,
    oc_send,
    oc_recv,
    ox_send,
    ox_recv,
    oz_send,
    oz_recv,
    eo,
    eo_recv,
    w_sem,
    send_sem,
    recv_sem,
):
    y = lax.axis_index("ctx")
    e = lax.axis_index("exp")
    z, x, k = e // 4, (e // 2) % 2, e % 2
    width = mixed_out.shape[1]
    half = width // 2
    cols = half // PROJ_PARTS
    ff = hidden.shape[2]
    ff_cols = ff // FF_PARTS
    out_half = width // 4
    out_cols = out_half // OUT_PARTS
    tokens = queries.shape[0]

    def device(yy, zz, xx, kk):
        return (yy, zz * 4 + xx * 2 + kk)

    other_core = device(y, z, x, 1 - k)
    x_next = device(y, z, 1 - x, k)
    y_next = device(1 - y, z, x, k)
    partners = [other_core, x_next]
    for dy in range(2):
        for dz in range(4):
            if dy or dz:
                partners.append(device((y + dy) % 2, (z + dz) % 4, x, k))

    weight_copies = {}

    def fetch(name, src, dst):
        copy = pltpu.make_async_copy(src, dst, w_sem.at[len(weight_copies)])
        weight_copies[name] = copy
        copy.start()

    fetch("wo", wo_hbm, wo)

    barrier = pltpu.get_barrier_semaphore()
    for partner in partners:
        pl.semaphore_signal(barrier, inc=1, device_id=partner, device_id_type=pl.DeviceIdType.MESH)

    kvh = e * (queries.shape[1] // HEAD_WIDTH) // (QUERY_HEAD_COUNT // KEY_VALUE_HEADS)
    kv_cols = pl.ds(pl.multiple_of(kvh * HEAD_WIDTH, HEAD_WIDTH), HEAD_WIDTH)
    kv[y, 0] = keys[:, kv_cols]
    kv[y, 1] = values[:, kv_cols]
    res[k] = residual[...].astype(F32)
    lanes = lax.broadcasted_iota(jnp.int32, (expert_ids.shape[0], EXTRA), 1) % 64
    gate_rows = jnp.zeros(lanes.shape, F32)
    for slot in range(expert_ids.shape[1]):
        gate_rows += jnp.where(
            expert_ids[:, slot : slot + 1] == lanes, expert_gates[:, slot : slot + 1], 0.0
        )
    table[k] = gate_rows

    pl.semaphore_wait(barrier, len(partners))

    sent = []

    def send(src, dst, to):
        number = len(sent)
        copy = pltpu.make_async_remote_copy(
            src_ref=src,
            dst_ref=dst,
            send_sem=send_sem.at[number],
            recv_sem=recv_sem.at[number],
            device_id=to,
            device_id_type=pl.DeviceIdType.MESH,
        )
        copy.start()
        sent.append(copy)
        return copy

    kv_copy = send(kv.at[y], kv.at[y], y_next)
    res_copy = send(res.at[k], res.at[k], other_core)
    table_copy = send(table.at[k], table.at[k], other_core)
    fetch("wg", wg_hbm.at[0], wg)
    fetch("wu", wu_hbm.at[0], wu)
    fetch("wd", wd_hbm.at[0], wd)

    kv_copy.wait_recv()
    key_all = kv[:, 0].reshape(2 * tokens, HEAD_WIDTH)
    value_all = kv[:, 1].reshape(2 * tokens, HEAD_WIDTH)
    shape = (tokens, 2 * tokens)
    allowed = lax.broadcasted_iota(jnp.int32, shape, 1) <= y * tokens + lax.broadcasted_iota(
        jnp.int32, shape, 0
    )
    scale = 1.0 / HEAD_WIDTH**0.5
    for head in range(queries.shape[1] // HEAD_WIDTH):
        span = slice(head * HEAD_WIDTH, (head + 1) * HEAD_WIDTH)
        scores = (
            lax.dot_general(
                queries[:, span], key_all, (((1,), (1,)), ((), ())), preferred_element_type=F32
            )
            * scale
        )
        scores = jnp.where(allowed, scores, neg_large)
        weights = jnp.where(
            allowed, jnp.exp(scores - jnp.max(scores, axis=1, keepdims=True)), 0.0
        )
        total = jnp.sum(weights, axis=1, keepdims=True)
        numer = jnp.dot(weights.astype(BF), value_all, preferred_element_type=F32)
        heads[:, span] = (numer / total).astype(BF)

    def columns(which, part, span, size):
        return pl.ds(pl.multiple_of(which * span + part * size, size), size)

    weight_copies["wo"].wait()
    to_core = []
    for part in range(PROJ_PARTS):
        piece = jnp.dot(
            heads[...], wo[:, columns(1 - k, part, half, cols)], preferred_element_type=F32
        )
        pc_send[part] = piece.astype(BF)
        to_core.append(send(pc_send.at[part], pc_recv.at[part], other_core))
    to_x = []
    for part in range(PROJ_PARTS):
        piece = jnp.dot(
            heads[...], wo[:, columns(k, part, half, cols)], preferred_element_type=F32
        )
        to_core[part].wait_recv()
        piece = (piece + pc_recv[part].astype(F32)).astype(BF)
        for chip in range(tokens // ROWS):
            px_send[part, chip % 2, chip // 2] = piece[chip * ROWS : (chip + 1) * ROWS]
        to_x.append(send(px_send.at[part, 1 - x], px_recv.at[part], x_next))
    to_z = []
    for part in range(PROJ_PARTS):
        to_x[part].wait_recv()
        pz_send[part] = (px_send[part, x].astype(F32) + px_recv[part].astype(F32)).astype(BF)
        for dz in range(1, 4):
            zz = (z + dz) % 4
            to_z.append(
                send(pz_send.at[part, zz], pz_recv.at[part, dz - 1], device(y, zz, x, k))
            )
    back = []
    for part in range(PROJ_PARTS):
        piece = pz_send[part, z].astype(F32)
        for dz in range(1, 4):
            to_z[part * 3 + dz - 1].wait_recv()
            piece += pz_recv[part, dz - 1].astype(F32)
        place = columns(k, part, half, cols)
        proj[:, place] = piece
        back.append(send(proj.at[:, place], proj.at[:, place], other_core))

    res_copy.wait_recv()
    table_copy.wait_recv()
    for copy in back:
        copy.wait_recv()
    stream = (proj[...] + res[...].reshape(ROWS, width)).astype(BF).astype(F32)
    mean_sq = jnp.mean(stream * stream, axis=1, keepdims=True)
    normed = (stream * lax.rsqrt(mean_sq + eps_norm) * norm_gain[...]).astype(BF)
    gates = table[...].reshape(ROWS, EXTRA)
    gate_high = gates.astype(BF).astype(F32)
    gate_lane = lax.broadcasted_iota(jnp.int32, gates.shape, 1)
    gates = jnp.where(gate_lane < 64, gate_high, gates - gate_high).astype(BF)

    def block(xx, yy, zz):
        return (xx * 2 + yy) * 4 + zz

    own = block(x, y, z)
    for side in range(2):
        rows_all[side, own, :, :half] = normed[:, side * half : (side + 1) * half]
        rows_all[side, own, :, half:] = gates

    def pass_on(number, to):
        place = rows_all.at[k, number]
        return send(place, place, to)

    y1, x1 = y + k * (1 - 2 * y), x + (1 - k) * (1 - 2 * x)
    y2, x2 = y + (1 - k) * (1 - 2 * y), x + k * (1 - 2 * x)
    first_to, second_to = device(y1, z, x1, k), device(y2, z, x2, k)
    along_z = [
        pass_on(own, device(y, (z + dz) % 4, x, k)) for dz in range(1, 4)
    ]
    first, second, second_far, cross = [], [], [], []
    first.append(pass_on(own, first_to))
    second.append(pass_on(own, second_to))
    mixed_rows[...] = stream.reshape(2, ROWS // 2, width)
    mixed_out[...] = mixed_rows[k].astype(BF)
    for i in range(1, 4):
        along_z[i - 1].wait_recv()
        number = block(x, y, (z + 4 - i) % 4)
        first.append(pass_on(number, first_to))
        second.append(pass_on(number, second_to))
        cross.append(pass_on(number, other_core))
    for i in range(4):
        first[i].wait_recv()
        number = block(x1, y1, (z + 4 - i) % 4)
        second_far.append(pass_on(number, second_to))
        cross.append(pass_on(number, other_core))
    for i in range(4):
        second[i].wait_recv()
        cross.append(pass_on(block(x2, y2, (z + 4 - i) % 4), other_core))
    for i in range(4):
        second_far[i].wait_recv()
        cross.append(pass_on(block(1 - x, 1 - y, (z + 4 - i) % 4), other_core))
    weight_copies["wg"].wait()
    weight_copies["wu"].wait()
    for copy in cross:
        copy.wait_recv()

    all_tokens = rows_all.shape[1] * ROWS
    across = []
    for part in range(FF_PARTS):
        span = slice(part * ff_cols, (part + 1) * ff_cols)
        gate = jnp.zeros((all_tokens, ff_cols), F32)
        upper = jnp.zeros((all_tokens, ff_cols), F32)
        for side in range(2):
            rows = rows_all[side, :, :, :half].reshape(all_tokens, half)
            depth = slice(side * half, (side + 1) * half)
            gate += jnp.dot(rows, wg[depth, span], preferred_element_type=F32)
            upper += jnp.dot(rows, wu[depth, span], preferred_element_type=F32)
        hidden[y, :, span] = (gate / (1.0 + jnp.exp(-gate)) * upper).astype(BF)
        place = hidden.at[y, :, span]
        across.append(send(place, place, y_next))
    picked = rows_all[0, :, :, half:].reshape(all_tokens, EXTRA).astype(F32)
    picked_lane = lax.broadcasted_iota(jnp.int32, picked.shape, 1) % 64
    share = jnp.sum(jnp.where(picked_lane == e, picked, 0.0), axis=1, keepdims=True)
    weight_copies["wd"].wait()
    for copy in across:
        copy.wait_recv()

    def down(which, part):
        place = columns(which, part, out_half, out_cols)
        result = jnp.dot(hidden[0], wd[:ff, place], preferred_element_type=F32)
        result += jnp.dot(hidden[1], wd[ff:, place], preferred_element_type=F32)
        return result * share

    to_core, to_x, to_z = [], [], []
    for part in range(OUT_PARTS):
        oc_send[part] = down(1 - k, part).astype(BF)
        to_core.append(send(oc_send.at[part], oc_recv.at[part], other_core))
    for part in range(OUT_PARTS):
        piece = down(k, part)
        to_core[part].wait_recv()
        piece = (piece + oc_recv[part].astype(F32)).astype(BF)
        ox_send[part] = piece.reshape(2, 8, ROWS, out_cols)
        to_x.append(send(ox_send.at[part, 1 - x], ox_recv.at[part], x_next))
    for part in range(OUT_PARTS):
        to_x[part].wait_recv()
        oz_send[part] = (ox_send[part, x].astype(F32) + ox_recv[part].astype(F32)).astype(BF)
        for dy in range(2):
            for dz in range(4):
                if dy or dz:
                    yy, zz = (y + dy) % 2, (z + dz) % 4
                    to_z.append(
                        send(
                            oz_send.at[part, yy * 4 + zz],
                            oz_recv.at[part, dy * 4 + dz],
                            device(yy, zz, x, k),
                        )
                    )
                else:
                    to_z.append(None)
    back = []
    for part in range(OUT_PARTS):
        for dy in range(2):
            piece = None
            for dz in range(4):
                copy = to_z[part * 8 + dy * 4 + dz]
                if copy is None:
                    piece = oz_send[part, y * 4 + z].astype(F32)
                    continue
                copy.wait_recv()
                came = oz_recv[part, dy * 4 + dz].astype(F32)
                piece = came if piece is None else piece + came
            side = y + dy * (1 - 2 * y)
            place = columns(side * 2 + k, part, out_half, out_cols)
            eo[:, :, place] = piece.reshape(2, ROWS // 2, out_cols)
            back.append(send(eo.at[1 - k, :, place], eo_recv.at[:, place], other_core))
    for part in range(OUT_PARTS):
        for side in range(2):
            place = columns(side * 2 + k, part, out_half, out_cols)
            experts_out[:, place] = eo[k, :, place].astype(BF)
    for copy in back:
        copy.wait_recv()
    for part in range(OUT_PARTS):
        for side in range(2):
            place = columns(side * 2 + 1 - k, part, out_half, out_cols)
            experts_out[:, place] = eo_recv[:, place].astype(BF)
    for copy in sent:
        copy.wait_send()


def layer_on_device(
    queries,
    keys,
    values,
    residual,
    out_weight,
    norm_gain,
    expert_ids,
    expert_gates,
    w_gate,
    w_up,
    w_down,
):
    tokens, head_cols = queries.shape
    own_rows, width = residual.shape
    ff = w_gate.shape[2]
    half = width // 2
    cols = half // PROJ_PARTS
    out_cols = width // 4 // OUT_PARTS
    all_tokens = 2 * tokens
    vmem = pl.BlockSpec(memory_space=pltpu.VMEM)
    hbm = pl.BlockSpec(memory_space=pl.ANY)
    scratch = [
        pltpu.VMEM(out_weight.shape, BF),
        pltpu.VMEM(w_gate.shape[1:], BF),
        pltpu.VMEM(w_up.shape[1:], BF),
        pltpu.VMEM(w_down.shape[1:], BF),
        pltpu.VMEM((2, 2, tokens, HEAD_WIDTH), BF),
        pltpu.VMEM((2, own_rows, width), F32),
        pltpu.VMEM((2, own_rows, EXTRA), F32),
        pltpu.VMEM((tokens, head_cols), BF),
        pltpu.VMEM((PROJ_PARTS, tokens, cols), BF),
        pltpu.VMEM((PROJ_PARTS, tokens, cols), BF),
        pltpu.VMEM((PROJ_PARTS, 2, 4, ROWS, cols), BF),
        pltpu.VMEM((PROJ_PARTS, 4, ROWS, cols), BF),
        pltpu.VMEM((PROJ_PARTS, 4, ROWS, cols), BF),
        pltpu.VMEM((PROJ_PARTS, 3, ROWS, cols), BF),
        pltpu.VMEM((ROWS, width), F32),
        pltpu.VMEM((2, own_rows, width), F32),
        pltpu.VMEM((2, 16, ROWS, half + EXTRA), BF),
        pltpu.VMEM((2, all_tokens, ff), BF),
        pltpu.VMEM((OUT_PARTS, all_tokens, out_cols), BF),
        pltpu.VMEM((OUT_PARTS, all_tokens, out_cols), BF),
        pltpu.VMEM((OUT_PARTS, 2, 8, ROWS, out_cols), BF),
        pltpu.VMEM((OUT_PARTS, 8, ROWS, out_cols), BF),
        pltpu.VMEM((OUT_PARTS, 8, ROWS, out_cols), BF),
        pltpu.VMEM((OUT_PARTS, 8, ROWS, out_cols), BF),
        pltpu.VMEM((2, own_rows, width), F32),
        pltpu.VMEM((own_rows, width), F32),
        pltpu.SemaphoreType.DMA((16,)),
        pltpu.SemaphoreType.DMA((96,)),
        pltpu.SemaphoreType.DMA((96,)),
    ]
    flops = 2 * all_tokens * width * ff * 4 + 2 * tokens * head_cols * width
    return pl.pallas_call(
        layer_kernel,
        out_shape=[jax.ShapeDtypeStruct((own_rows, width), BF)] * 2,
        in_specs=[vmem] * 7 + [hbm] * 4,
        out_specs=[vmem] * 2,
        scratch_shapes=scratch,
        compiler_params=pltpu.CompilerParams(
            collective_id=0, has_side_effects=True, vmem_limit_bytes=56 * 2**20
        ),
        cost_estimate=pl.CostEstimate(
            flops=flops, bytes_accessed=24 * 2**20, transcendentals=2**18
        ),
    )(
        queries,
        keys,
        values,
        residual,
        norm_gain.reshape(1, width),
        expert_ids,
        expert_gates,
        out_weight,
        w_gate,
        w_up,
        w_down,
    )


def solution(mesh):
    one_block = mesh.shape["ctx"] == 2 and mesh.shape["exp"] == 16
    return jax.shard_map(
        layer_on_device if one_block else on_device,
        mesh=mesh,
        in_specs=(
            P("ctx", "exp"),
            P("ctx", None),
            P("ctx", None),
            P(("ctx", "exp"), None),
            P("exp", None),
            P(),
            P(("ctx", "exp"), None),
            P(("ctx", "exp"), None),
            P("exp", None, "ctx"),
            P("exp", None, "ctx"),
            P("exp", None, "ctx"),
        ),
        out_specs=(P(("ctx", "exp"), None), P(("ctx", "exp"), None)),
        check_vma=False,
    )
```

```python
import jax
import jax.numpy as jnp
from jax import lax
from jax.experimental import pallas as pl
from jax.experimental.pallas import tpu as pltpu
from jax.sharding import PartitionSpec as P

QUERY_HEAD_COUNT = 64
KEY_VALUE_HEADS = 4
HEAD_WIDTH = 128


neg_large = -1e30
eps_norm = 1e-06


def shifted(value, axis, by):
    size = lax.axis_size(axis)
    pairs = [(i, i + by) for i in range(size) if 0 <= i + by < size]
    return lax.ppermute(value, axis, pairs)


def slot_numbers(expert_ids):
    tok_rows, top_count = expert_ids.shape
    flat_ids = expert_ids.reshape(-1)
    owner_row = jnp.arange(tok_rows * top_count, dtype=jnp.int32) // top_count
    earlier = (flat_ids[:, None] == flat_ids[None, :]) & (owner_row[None, :] < owner_row[:, None])
    return jnp.sum(earlier.astype(jnp.int32), axis=1).reshape(tok_rows, top_count)


def route_hits(expert_ids, slot_ids, expert_count, capacity):
    expert_hit = (
        expert_ids[None, None, :, :]
        == jnp.arange(expert_count, dtype=jnp.int32)[:, None, None, None]
    )
    slot_hit = (
        slot_ids[None, None, :, :] == jnp.arange(capacity, dtype=jnp.int32)[None, :, None, None]
    )
    return expert_hit & slot_hit


def expert_hidden(rows_block, gate_local, up_local):
    gate = jnp.dot(rows_block, gate_local, preferred_element_type=jnp.float32)
    upper = jnp.dot(rows_block, up_local, preferred_element_type=jnp.float32)
    return (jax.nn.silu(gate) * upper).astype(jnp.bfloat16)


def on_device(
    queries,
    keys,
    values,
    residual,
    out_weight,
    norm_gain,
    expert_ids,
    expert_gates,
    w_gate,
    w_up,
    w_down,
):
    tok_query = queries.shape[0]
    device_share = queries.shape[1] // HEAD_WIDTH
    ctx_pos = lax.axis_index("ctx")
    key_value_head = lax.axis_index("exp") * device_share // (QUERY_HEAD_COUNT // KEY_VALUE_HEADS)
    own_keys = lax.dynamic_slice_in_dim(keys, key_value_head * HEAD_WIDTH, HEAD_WIDTH, 1)
    own_values = lax.dynamic_slice_in_dim(values, key_value_head * HEAD_WIDTH, HEAD_WIDTH, 1)
    own_block = jnp.stack([own_keys, own_values])
    query_heads = queries.reshape(tok_query, device_share, HEAD_WIDTH)
    query_start = ctx_pos * tok_query
    query_pos = query_start + jnp.arange(tok_query, dtype=jnp.int32)
    scale = 1.0 / HEAD_WIDTH**0.5
    start_state = (
        jnp.full((device_share, tok_query), neg_large, jnp.float32),
        jnp.zeros((device_share, tok_query), jnp.float32),
        jnp.zeros((device_share, tok_query, HEAD_WIDTH), jnp.float32),
    )

    def attend(state_now, kv_piece, key_start):

        def compute(current):
            running_max, running_sum, weighted = current
            key_pos = key_start + jnp.arange(kv_piece.shape[1], dtype=jnp.int32)
            allowed = key_pos[None, :] <= query_pos[:, None]
            scores = (
                jnp.einsum(
                    "qhd,kd->hqk", query_heads, kv_piece[0], preferred_element_type=jnp.float32
                )
                * scale
            )
            scores = jnp.where(allowed[None], scores, neg_large)
            new_max = jnp.maximum(running_max, jnp.max(scores, axis=2))
            weights_blk = jnp.where(allowed[None], jnp.exp(scores - new_max[:, :, None]), 0.0)
            shrink = jnp.exp(running_max - new_max)
            new_sum = running_sum * shrink + jnp.sum(weights_blk, axis=2)
            added = jnp.einsum(
                "hqk,kd->hqd",
                weights_blk.astype(jnp.bfloat16),
                kv_piece[1],
                preferred_element_type=jnp.float32,
            )
            return (new_max, new_sum, weighted * shrink[:, :, None] + added)

        def unchanged(current):
            return current

        useful = (key_start >= 0) & (key_start <= query_start + tok_query - 1)
        return lax.cond(useful, compute, unchanged, state_now)

    ctx_count = lax.axis_size("ctx")
    state_now = attend(start_state, own_block, query_start)

    def cycle_turn(cycle_step, carried):
        state_cur, moving = carried
        moving = shifted(moving, "ctx", 1)
        source = ctx_pos - cycle_step
        return (attend(state_cur, moving, source * tok_query), moving)

    state_now, _ = lax.fori_loop(1, ctx_count, cycle_turn, (state_now, own_block))
    running_max, running_sum, weighted = state_now
    heads_done = (weighted / running_sum[:, :, None]).astype(jnp.bfloat16)
    heads_done = jnp.transpose(heads_done, (1, 0, 2)).reshape(tok_query, device_share * HEAD_WIDTH)
    tok_rows, top_count = expert_ids.shape
    projected = lax.psum_scatter(
        jnp.dot(heads_done, out_weight, preferred_element_type=jnp.float32).astype(jnp.bfloat16),
        "exp",
        scatter_dimension=0,
        tiled=True,
    ).astype(jnp.float32)
    mixed = (residual.astype(jnp.float32) + projected).astype(jnp.bfloat16)
    stream = mixed.astype(jnp.float32)
    mean_sq = jnp.mean(stream * stream, axis=1, keepdims=True)
    normed = (stream * lax.rsqrt(mean_sq + eps_norm) * norm_gain[None, :]).astype(jnp.bfloat16)
    expert_count = lax.axis_size("exp")
    ctx_count = lax.axis_size("ctx")
    capacity = min(tok_rows, 2 * tok_rows * top_count // expert_count)
    slot_ids = slot_numbers(expert_ids)
    hits = route_hits(expert_ids, slot_ids, expert_count, capacity)
    send_table = jnp.any(hits, axis=3).astype(jnp.bfloat16)
    gate_local = w_gate[0]
    up_local = w_up[0]
    down_local = w_down[0]
    width = normed.shape[1]
    outgoing = jnp.einsum(
        "ecm,md->ecd", send_table, normed, preferred_element_type=jnp.float32
    ).astype(jnp.bfloat16)
    arrived = lax.all_to_all(outgoing, "exp", split_axis=0, concat_axis=0, tiled=True)
    local_rows = arrived.reshape(-1, width)
    hidden = expert_hidden(
        lax.all_gather(local_rows, "ctx", axis=0, tiled=True), gate_local, up_local
    )
    expert_result = jnp.dot(
        lax.all_gather(hidden, "ctx", axis=1, tiled=True),
        down_local,
        preferred_element_type=jnp.float32,
    ).astype(jnp.bfloat16)
    expert_result = expert_result.reshape(ctx_count, expert_count, capacity, down_local.shape[1])
    returned = lax.all_to_all(
        lax.all_to_all(expert_result, "ctx", split_axis=0, concat_axis=3, tiled=True),
        "exp",
        split_axis=1,
        concat_axis=0,
        tiled=True,
    )
    returned = returned.reshape(expert_count, capacity, width)
    mix_table = jnp.sum(jnp.where(hits, expert_gates[None, None, :, :], 0.0), axis=3)
    experts_out = jnp.einsum(
        "ecm,ecd->md", mix_table, returned.astype(jnp.float32), precision=lax.Precision.HIGHEST
    )
    return (mixed, experts_out.astype(jnp.bfloat16))


BF = jnp.bfloat16
F32 = jnp.float32
ROWS = 16
EXTRA = 128
PROJ_PARTS = 4
FF_PARTS = 3
OUT_PARTS = 2


def layer_kernel(
    queries,
    keys,
    values,
    residual,
    norm_gain,
    expert_ids,
    expert_gates,
    wo_hbm,
    wg_hbm,
    wu_hbm,
    wd_hbm,
    mixed_out,
    experts_out,
    wo,
    wg,
    wu,
    wd,
    kv,
    res,
    table,
    heads,
    pc_send,
    pc_recv,
    px_send,
    px_recv,
    pz_send,
    pz_recv,
    proj,
    mixed_rows,
    rows_all,
    hidden,
    oc_send,
    oc_recv,
    ox_send,
    ox_recv,
    oz_send,
    oz_recv,
    eo,
    eo_recv,
    w_sem,
    send_sem,
    recv_sem,
):
    y = lax.axis_index("ctx")
    e = lax.axis_index("exp")
    z, x, k = e // 4, (e // 2) % 2, e % 2
    width = mixed_out.shape[1]
    half = width // 2
    cols = half // PROJ_PARTS
    ff = hidden.shape[3]
    ff_cols = ff // FF_PARTS
    out_half = width // 4
    out_cols = out_half // OUT_PARTS
    tokens = queries.shape[0]

    def device(yy, zz, xx, kk):
        return (yy, zz * 4 + xx * 2 + kk)

    zs = (z, z + 1 - 2 * (z % 2), (z + 2) % 4, 3 - z)
    other_core = device(y, z, x, 1 - k)
    x_next = device(y, z, 1 - x, k)
    y_next = device(1 - y, z, x, k)
    partners = [other_core, x_next]
    for dy in range(2):
        for dz in range(4):
            if dy or dz:
                partners.append(device((y + dy) % 2, (z + dz) % 4, x, k))

    weight_copies = {}

    def fetch(name, src, dst):
        copy = pltpu.make_async_copy(src, dst, w_sem.at[len(weight_copies)])
        weight_copies[name] = copy
        copy.start()

    fetch("wo", wo_hbm, wo)

    barrier = pltpu.get_barrier_semaphore()
    for partner in partners:
        pl.semaphore_signal(barrier, inc=1, device_id=partner, device_id_type=pl.DeviceIdType.MESH)

    kvh = e * (queries.shape[1] // HEAD_WIDTH) // (QUERY_HEAD_COUNT // KEY_VALUE_HEADS)
    kv_cols = pl.ds(pl.multiple_of(kvh * HEAD_WIDTH, HEAD_WIDTH), HEAD_WIDTH)
    kv[y, 0] = keys[:, kv_cols]
    kv[y, 1] = values[:, kv_cols]
    res[k] = residual[...].astype(F32)
    lanes = lax.broadcasted_iota(jnp.int32, (expert_ids.shape[0], EXTRA), 1) % 64
    gate_rows = jnp.zeros(lanes.shape, F32)
    for slot in range(expert_ids.shape[1]):
        gate_rows += jnp.where(
            expert_ids[:, slot : slot + 1] == lanes, expert_gates[:, slot : slot + 1], 0.0
        )
    table[k] = gate_rows

    pl.semaphore_wait(barrier, len(partners))

    sent = []

    def send(src, dst, to):
        number = len(sent)
        copy = pltpu.make_async_remote_copy(
            src_ref=src,
            dst_ref=dst,
            send_sem=send_sem.at[number],
            recv_sem=recv_sem.at[number],
            device_id=to,
            device_id_type=pl.DeviceIdType.MESH,
        )
        copy.start()
        sent.append(copy)
        return copy

    kv_copy = send(kv.at[y], kv.at[y], y_next)
    res_copy = send(res.at[k], res.at[k], other_core)
    table_copy = send(table.at[k], table.at[k], other_core)
    fetch("wg", wg_hbm.at[0], wg)
    fetch("wu", wu_hbm.at[0], wu)
    fetch("wd", wd_hbm.at[0], wd)

    kv_copy.wait_recv()
    key_all = kv[:, 0].reshape(2 * tokens, HEAD_WIDTH)
    value_all = kv[:, 1].reshape(2 * tokens, HEAD_WIDTH)
    shape = (tokens, 2 * tokens)
    allowed = lax.broadcasted_iota(jnp.int32, shape, 1) <= y * tokens + lax.broadcasted_iota(
        jnp.int32, shape, 0
    )
    scale = 1.0 / HEAD_WIDTH**0.5
    for head in range(queries.shape[1] // HEAD_WIDTH):
        span = slice(head * HEAD_WIDTH, (head + 1) * HEAD_WIDTH)
        scores = (
            lax.dot_general(
                queries[:, span], key_all, (((1,), (1,)), ((), ())), preferred_element_type=F32
            )
            * scale
        )
        scores = jnp.where(allowed, scores, neg_large)
        weights = jnp.where(
            allowed, jnp.exp(scores - jnp.max(scores, axis=1, keepdims=True)), 0.0
        )
        total = jnp.sum(weights, axis=1, keepdims=True)
        numer = jnp.dot(weights.astype(BF), value_all, preferred_element_type=F32)
        heads[:, span] = (numer / total).astype(BF)

    def columns(which, part, span, size):
        return pl.ds(pl.multiple_of(which * span + part * size, size), size)

    weight_copies["wo"].wait()
    to_core = []
    for part in range(PROJ_PARTS):
        piece = jnp.dot(
            heads[...], wo[:, columns(1 - k, part, half, cols)], preferred_element_type=F32
        )
        pc_send[part] = piece.astype(BF)
        to_core.append(send(pc_send.at[part], pc_recv.at[part], other_core))
    to_x = []
    for part in range(PROJ_PARTS):
        piece = jnp.dot(
            heads[...], wo[:, columns(k, part, half, cols)], preferred_element_type=F32
        )
        to_core[part].wait_recv()
        piece = (piece + pc_recv[part].astype(F32)).astype(BF)
        for chip in range(tokens // ROWS):
            px_send[part, chip % 2, chip // 2] = piece[chip * ROWS : (chip + 1) * ROWS]
        to_x.append(send(px_send.at[part, 1 - x], px_recv.at[part], x_next))
    to_z = []
    for part in range(PROJ_PARTS):
        to_x[part].wait_recv()
        pz_send[part] = (px_send[part, x].astype(F32) + px_recv[part].astype(F32)).astype(BF)
        for dz in range(1, 4):
            zz = (z + dz) % 4
            to_z.append(
                send(pz_send.at[part, zz], pz_recv.at[part, dz - 1], device(y, zz, x, k))
            )
    back = []
    for part in range(PROJ_PARTS):
        piece = pz_send[part, z].astype(F32)
        for dz in range(1, 4):
            to_z[part * 3 + dz - 1].wait_recv()
            piece += pz_recv[part, dz - 1].astype(F32)
        place = columns(k, part, half, cols)
        proj[:, place] = piece
        back.append(send(proj.at[:, place], proj.at[:, place], other_core))

    res_copy.wait_recv()
    table_copy.wait_recv()
    for copy in back:
        copy.wait_recv()
    stream = (proj[...] + res[...].reshape(ROWS, width)).astype(BF).astype(F32)
    mean_sq = jnp.mean(stream * stream, axis=1, keepdims=True)
    normed = (stream * lax.rsqrt(mean_sq + eps_norm) * norm_gain[...]).astype(BF)
    gates = table[...].reshape(ROWS, EXTRA)
    gate_high = gates.astype(BF).astype(F32)
    gate_lane = lax.broadcasted_iota(jnp.int32, gates.shape, 1)
    gates = jnp.where(gate_lane < 64, gate_high, gates - gate_high).astype(BF)

    def block(xx, yy, zz):
        return ((zz // 2) * 4 + xx * 2 + yy) * 2 + zz % 2

    own = block(x, y, z)
    for side in range(2):
        rows_all[side, own, :, :half] = normed[:, side * half : (side + 1) * half]
        rows_all[side, own, :, half:] = gates

    def pass_on(number, to):
        place = rows_all.at[k, number]
        return send(place, place, to)

    y1, x1 = y + k * (1 - 2 * y), x + (1 - k) * (1 - 2 * x)
    y2, x2 = y + (1 - k) * (1 - 2 * y), x + k * (1 - 2 * x)
    first_to, second_to = device(y1, z, x1, k), device(y2, z, x2, k)
    along_z = [pass_on(own, device(y, zs[1], x, k))]
    first, second, second_far = {}, {}, {}
    cross = [[], []]
    first[0] = pass_on(own, first_to)
    second[0] = pass_on(own, second_to)
    along_z += [pass_on(own, device(y, zz, x, k)) for zz in zs[2:]]
    mixed_rows[...] = stream.reshape(2, ROWS // 2, width)
    mixed_out[...] = mixed_rows[k].astype(BF)

    def take_z(i):
        along_z[i - 1].wait_recv()
        number = block(x, y, zs[i])
        first[i] = pass_on(number, first_to)
        second[i] = pass_on(number, second_to)
        cross[i // 2].append(pass_on(number, other_core))

    def take_first(i):
        first[i].wait_recv()
        number = block(x1, y1, zs[i])
        second_far[i] = pass_on(number, second_to)
        cross[i // 2].append(pass_on(number, other_core))

    def take_second(i):
        second[i].wait_recv()
        cross[i // 2].append(pass_on(block(x2, y2, zs[i]), other_core))

    def take_far(i):
        second_far[i].wait_recv()
        cross[i // 2].append(pass_on(block(1 - x, 1 - y, zs[i]), other_core))

    chunk_tokens = tokens
    chunk_blocks = chunk_tokens // ROWS
    across = [[], []]

    def chunk_rows(chunk):
        pair = z // 2 + chunk * (1 - 2 * (z // 2))
        return pl.ds(pair * chunk_blocks, chunk_blocks)

    def expert_up(chunk, part):
        span = slice(part * ff_cols, (part + 1) * ff_cols)
        gate = jnp.zeros((chunk_tokens, ff_cols), F32)
        upper = jnp.zeros((chunk_tokens, ff_cols), F32)
        for side in range(2):
            rows = rows_all[side, chunk_rows(chunk), :, :half].reshape(chunk_tokens, half)
            depth = slice(side * half, (side + 1) * half)
            gate += jnp.dot(rows, wg[depth, span], preferred_element_type=F32)
            upper += jnp.dot(rows, wu[depth, span], preferred_element_type=F32)
        hidden[chunk, y, :, span] = (gate / (1.0 + jnp.exp(-gate)) * upper).astype(BF)
        place = hidden.at[chunk, y, :, span]
        across[chunk].append(send(place, place, y_next))

    take_z(1)
    take_first(0)
    take_second(0)
    take_z(2)
    take_first(1)
    take_second(1)
    take_z(3)
    take_far(0)
    take_far(1)
    weight_copies["wg"].wait()
    weight_copies["wu"].wait()
    for copy in cross[0]:
        copy.wait_recv()
    expert_up(0, 0)
    take_first(2)
    take_second(2)
    for part in range(1, FF_PARTS):
        expert_up(0, part)
        if part == 1:
            take_first(3)
            take_second(3)
    take_far(2)
    take_far(3)
    for copy in cross[1]:
        copy.wait_recv()
    for part in range(FF_PARTS):
        expert_up(1, part)

    shares = []
    for chunk in range(2):
        picked = rows_all[0, chunk_rows(chunk), :, half:].reshape(chunk_tokens, EXTRA).astype(F32)
        picked_lane = lax.broadcasted_iota(jnp.int32, picked.shape, 1) % 64
        shares.append(jnp.sum(jnp.where(picked_lane == e, picked, 0.0), axis=1, keepdims=True))
    weight_copies["wd"].wait()

    def down(chunk, which, part):
        place = columns(which, part, out_half, out_cols)
        result = jnp.dot(hidden[chunk, 0], wd[:ff, place], preferred_element_type=F32)
        result += jnp.dot(hidden[chunk, 1], wd[ff:, place], preferred_element_type=F32)
        return result * shares[chunk]

    to_x, to_z = {}, {}

    def outputs_to_x(chunk):
        for copy in across[chunk]:
            copy.wait_recv()
        to_core = []
        for part in range(OUT_PARTS):
            oc_send[chunk, part] = down(chunk, 1 - k, part).astype(BF)
            to_core.append(send(oc_send.at[chunk, part], oc_recv.at[chunk, part], other_core))
        for part in range(OUT_PARTS):
            piece = down(chunk, k, part)
            to_core[part].wait_recv()
            piece = (piece + oc_recv[chunk, part].astype(F32)).astype(BF)
            ox_send[chunk, part] = piece.reshape(2, 2, 2, ROWS, out_cols)
            to_x[chunk, part] = send(
                ox_send.at[chunk, part, 1 - x], ox_recv.at[chunk, part], x_next
            )

    def outputs_to_z(chunk):
        for part in range(OUT_PARTS):
            to_x[chunk, part].wait_recv()
            oz_send[chunk, part] = (
                ox_send[chunk, part, x].astype(F32) + ox_recv[chunk, part].astype(F32)
            ).astype(BF)
            for dy in range(2):
                for dz in (2 * chunk, 2 * chunk + 1):
                    if dy or dz:
                        yy = y + dy * (1 - 2 * y)
                        to_z[part, dy, dz] = send(
                            oz_send.at[chunk, part, yy, zs[dz] % 2],
                            oz_recv.at[part, dy * 4 + dz],
                            device(yy, zs[dz], x, k),
                        )

    outputs_to_x(0)
    outputs_to_z(0)
    outputs_to_x(1)
    outputs_to_z(1)
    back = []
    for part in range(OUT_PARTS):
        for dy in range(2):
            piece = None
            for dz in range(4):
                if (part, dy, dz) not in to_z:
                    piece = oz_send[0, part, y, z % 2].astype(F32)
                    continue
                to_z[part, dy, dz].wait_recv()
                came = oz_recv[part, dy * 4 + dz].astype(F32)
                piece = came if piece is None else piece + came
            side = y + dy * (1 - 2 * y)
            place = columns(side * 2 + k, part, out_half, out_cols)
            eo[:, :, place] = piece.reshape(2, ROWS // 2, out_cols)
            back.append(send(eo.at[1 - k, :, place], eo_recv.at[:, place], other_core))
    for part in range(OUT_PARTS):
        for side in range(2):
            place = columns(side * 2 + k, part, out_half, out_cols)
            experts_out[:, place] = eo[k, :, place].astype(BF)
    for copy in back:
        copy.wait_recv()
    for part in range(OUT_PARTS):
        for side in range(2):
            place = columns(side * 2 + 1 - k, part, out_half, out_cols)
            experts_out[:, place] = eo_recv[:, place].astype(BF)
    for copy in sent:
        copy.wait_send()


def layer_on_device(
    queries,
    keys,
    values,
    residual,
    out_weight,
    norm_gain,
    expert_ids,
    expert_gates,
    w_gate,
    w_up,
    w_down,
):
    tokens, head_cols = queries.shape
    own_rows, width = residual.shape
    ff = w_gate.shape[2]
    half = width // 2
    cols = half // PROJ_PARTS
    out_cols = width // 4 // OUT_PARTS
    all_tokens = 2 * tokens
    vmem = pl.BlockSpec(memory_space=pltpu.VMEM)
    hbm = pl.BlockSpec(memory_space=pl.ANY)
    scratch = [
        pltpu.VMEM(out_weight.shape, BF),
        pltpu.VMEM(w_gate.shape[1:], BF),
        pltpu.VMEM(w_up.shape[1:], BF),
        pltpu.VMEM(w_down.shape[1:], BF),
        pltpu.VMEM((2, 2, tokens, HEAD_WIDTH), BF),
        pltpu.VMEM((2, own_rows, width), F32),
        pltpu.VMEM((2, own_rows, EXTRA), F32),
        pltpu.VMEM((tokens, head_cols), BF),
        pltpu.VMEM((PROJ_PARTS, tokens, cols), BF),
        pltpu.VMEM((PROJ_PARTS, tokens, cols), BF),
        pltpu.VMEM((PROJ_PARTS, 2, 4, ROWS, cols), BF),
        pltpu.VMEM((PROJ_PARTS, 4, ROWS, cols), BF),
        pltpu.VMEM((PROJ_PARTS, 4, ROWS, cols), BF),
        pltpu.VMEM((PROJ_PARTS, 3, ROWS, cols), BF),
        pltpu.VMEM((ROWS, width), F32),
        pltpu.VMEM((2, own_rows, width), F32),
        pltpu.VMEM((2, 16, ROWS, half + EXTRA), BF),
        pltpu.VMEM((2, 2, tokens, ff), BF),
        pltpu.VMEM((2, OUT_PARTS, tokens, out_cols), BF),
        pltpu.VMEM((2, OUT_PARTS, tokens, out_cols), BF),
        pltpu.VMEM((2, OUT_PARTS, 2, 2, 2, ROWS, out_cols), BF),
        pltpu.VMEM((2, OUT_PARTS, 2, 2, ROWS, out_cols), BF),
        pltpu.VMEM((2, OUT_PARTS, 2, 2, ROWS, out_cols), BF),
        pltpu.VMEM((OUT_PARTS, 8, ROWS, out_cols), BF),
        pltpu.VMEM((2, own_rows, width), F32),
        pltpu.VMEM((own_rows, width), F32),
        pltpu.SemaphoreType.DMA((16,)),
        pltpu.SemaphoreType.DMA((96,)),
        pltpu.SemaphoreType.DMA((96,)),
    ]
    flops = 2 * all_tokens * width * ff * 4 + 2 * tokens * head_cols * width
    return pl.pallas_call(
        layer_kernel,
        out_shape=[jax.ShapeDtypeStruct((own_rows, width), BF)] * 2,
        in_specs=[vmem] * 7 + [hbm] * 4,
        out_specs=[vmem] * 2,
        scratch_shapes=scratch,
        compiler_params=pltpu.CompilerParams(
            collective_id=0, has_side_effects=True, vmem_limit_bytes=56 * 2**20
        ),
        cost_estimate=pl.CostEstimate(
            flops=flops, bytes_accessed=24 * 2**20, transcendentals=2**18
        ),
    )(
        queries,
        keys,
        values,
        residual,
        norm_gain.reshape(1, width),
        expert_ids,
        expert_gates,
        out_weight,
        w_gate,
        w_up,
        w_down,
    )


def solution(mesh):
    one_block = mesh.shape["ctx"] == 2 and mesh.shape["exp"] == 16
    return jax.shard_map(
        layer_on_device if one_block else on_device,
        mesh=mesh,
        in_specs=(
            P("ctx", "exp"),
            P("ctx", None),
            P("ctx", None),
            P(("ctx", "exp"), None),
            P("exp", None),
            P(),
            P(("ctx", "exp"), None),
            P(("ctx", "exp"), None),
            P("exp", None, "ctx"),
            P("exp", None, "ctx"),
            P("exp", None, "ctx"),
        ),
        out_specs=(P(("ctx", "exp"), None), P(("ctx", "exp"), None)),
        check_vma=False,
    )
```

```python
import jax
import jax.numpy as jnp
from jax import lax
from jax.experimental import pallas as pl
from jax.experimental.pallas import tpu as pltpu
from jax.sharding import PartitionSpec as P

QUERY_HEAD_COUNT = 64
KEY_VALUE_HEADS = 4
HEAD_WIDTH = 128


neg_large = -1e30
eps_norm = 1e-06


def shifted(value, axis, by):
    size = lax.axis_size(axis)
    pairs = [(i, i + by) for i in range(size) if 0 <= i + by < size]
    return lax.ppermute(value, axis, pairs)


def slot_numbers(expert_ids):
    tok_rows, top_count = expert_ids.shape
    flat_ids = expert_ids.reshape(-1)
    owner_row = jnp.arange(tok_rows * top_count, dtype=jnp.int32) // top_count
    earlier = (flat_ids[:, None] == flat_ids[None, :]) & (owner_row[None, :] < owner_row[:, None])
    return jnp.sum(earlier.astype(jnp.int32), axis=1).reshape(tok_rows, top_count)


def route_hits(expert_ids, slot_ids, expert_count, capacity):
    expert_hit = (
        expert_ids[None, None, :, :]
        == jnp.arange(expert_count, dtype=jnp.int32)[:, None, None, None]
    )
    slot_hit = (
        slot_ids[None, None, :, :] == jnp.arange(capacity, dtype=jnp.int32)[None, :, None, None]
    )
    return expert_hit & slot_hit


def expert_hidden(rows_block, gate_local, up_local):
    gate = jnp.dot(rows_block, gate_local, preferred_element_type=jnp.float32)
    upper = jnp.dot(rows_block, up_local, preferred_element_type=jnp.float32)
    return (jax.nn.silu(gate) * upper).astype(jnp.bfloat16)


def on_device(
    queries,
    keys,
    values,
    residual,
    out_weight,
    norm_gain,
    expert_ids,
    expert_gates,
    w_gate,
    w_up,
    w_down,
):
    tok_query = queries.shape[0]
    device_share = queries.shape[1] // HEAD_WIDTH
    ctx_pos = lax.axis_index("ctx")
    key_value_head = lax.axis_index("exp") * device_share // (QUERY_HEAD_COUNT // KEY_VALUE_HEADS)
    own_keys = lax.dynamic_slice_in_dim(keys, key_value_head * HEAD_WIDTH, HEAD_WIDTH, 1)
    own_values = lax.dynamic_slice_in_dim(values, key_value_head * HEAD_WIDTH, HEAD_WIDTH, 1)
    own_block = jnp.stack([own_keys, own_values])
    query_heads = queries.reshape(tok_query, device_share, HEAD_WIDTH)
    query_start = ctx_pos * tok_query
    query_pos = query_start + jnp.arange(tok_query, dtype=jnp.int32)
    scale = 1.0 / HEAD_WIDTH**0.5
    start_state = (
        jnp.full((device_share, tok_query), neg_large, jnp.float32),
        jnp.zeros((device_share, tok_query), jnp.float32),
        jnp.zeros((device_share, tok_query, HEAD_WIDTH), jnp.float32),
    )

    def attend(state_now, kv_piece, key_start):

        def compute(current):
            running_max, running_sum, weighted = current
            key_pos = key_start + jnp.arange(kv_piece.shape[1], dtype=jnp.int32)
            allowed = key_pos[None, :] <= query_pos[:, None]
            scores = (
                jnp.einsum(
                    "qhd,kd->hqk", query_heads, kv_piece[0], preferred_element_type=jnp.float32
                )
                * scale
            )
            scores = jnp.where(allowed[None], scores, neg_large)
            new_max = jnp.maximum(running_max, jnp.max(scores, axis=2))
            weights_blk = jnp.where(allowed[None], jnp.exp(scores - new_max[:, :, None]), 0.0)
            shrink = jnp.exp(running_max - new_max)
            new_sum = running_sum * shrink + jnp.sum(weights_blk, axis=2)
            added = jnp.einsum(
                "hqk,kd->hqd",
                weights_blk.astype(jnp.bfloat16),
                kv_piece[1],
                preferred_element_type=jnp.float32,
            )
            return (new_max, new_sum, weighted * shrink[:, :, None] + added)

        def unchanged(current):
            return current

        useful = (key_start >= 0) & (key_start <= query_start + tok_query - 1)
        return lax.cond(useful, compute, unchanged, state_now)

    ctx_count = lax.axis_size("ctx")
    state_now = attend(start_state, own_block, query_start)

    def cycle_turn(cycle_step, carried):
        state_cur, moving = carried
        moving = shifted(moving, "ctx", 1)
        source = ctx_pos - cycle_step
        return (attend(state_cur, moving, source * tok_query), moving)

    state_now, _ = lax.fori_loop(1, ctx_count, cycle_turn, (state_now, own_block))
    running_max, running_sum, weighted = state_now
    heads_done = (weighted / running_sum[:, :, None]).astype(jnp.bfloat16)
    heads_done = jnp.transpose(heads_done, (1, 0, 2)).reshape(tok_query, device_share * HEAD_WIDTH)
    tok_rows, top_count = expert_ids.shape
    projected = lax.psum_scatter(
        jnp.dot(heads_done, out_weight, preferred_element_type=jnp.float32).astype(jnp.bfloat16),
        "exp",
        scatter_dimension=0,
        tiled=True,
    ).astype(jnp.float32)
    mixed = (residual.astype(jnp.float32) + projected).astype(jnp.bfloat16)
    stream = mixed.astype(jnp.float32)
    mean_sq = jnp.mean(stream * stream, axis=1, keepdims=True)
    normed = (stream * lax.rsqrt(mean_sq + eps_norm) * norm_gain[None, :]).astype(jnp.bfloat16)
    expert_count = lax.axis_size("exp")
    ctx_count = lax.axis_size("ctx")
    capacity = min(tok_rows, 2 * tok_rows * top_count // expert_count)
    slot_ids = slot_numbers(expert_ids)
    hits = route_hits(expert_ids, slot_ids, expert_count, capacity)
    send_table = jnp.any(hits, axis=3).astype(jnp.bfloat16)
    gate_local = w_gate[0]
    up_local = w_up[0]
    down_local = w_down[0]
    width = normed.shape[1]
    outgoing = jnp.einsum(
        "ecm,md->ecd", send_table, normed, preferred_element_type=jnp.float32
    ).astype(jnp.bfloat16)
    arrived = lax.all_to_all(outgoing, "exp", split_axis=0, concat_axis=0, tiled=True)
    local_rows = arrived.reshape(-1, width)
    hidden = expert_hidden(
        lax.all_gather(local_rows, "ctx", axis=0, tiled=True), gate_local, up_local
    )
    expert_result = jnp.dot(
        lax.all_gather(hidden, "ctx", axis=1, tiled=True),
        down_local,
        preferred_element_type=jnp.float32,
    ).astype(jnp.bfloat16)
    expert_result = expert_result.reshape(ctx_count, expert_count, capacity, down_local.shape[1])
    returned = lax.all_to_all(
        lax.all_to_all(expert_result, "ctx", split_axis=0, concat_axis=3, tiled=True),
        "exp",
        split_axis=1,
        concat_axis=0,
        tiled=True,
    )
    returned = returned.reshape(expert_count, capacity, width)
    mix_table = jnp.sum(jnp.where(hits, expert_gates[None, None, :, :], 0.0), axis=3)
    experts_out = jnp.einsum(
        "ecm,ecd->md", mix_table, returned.astype(jnp.float32), precision=lax.Precision.HIGHEST
    )
    return (mixed, experts_out.astype(jnp.bfloat16))


BF = jnp.bfloat16
F32 = jnp.float32
ROWS = 16
EXTRA = 128
PROJ_PARTS = 4
FF_PARTS = 3
OUT_PARTS = 2


def layer_kernel(
    queries,
    keys,
    values,
    residual,
    norm_gain,
    expert_ids,
    expert_gates,
    wo_hbm,
    wg_hbm,
    wu_hbm,
    wd_hbm,
    mixed_out,
    experts_out,
    wo,
    wg,
    wu,
    wd,
    kv,
    res,
    table,
    heads,
    pc_send,
    pc_recv,
    px_send,
    px_recv,
    pz_send,
    pz_recv,
    proj,
    mixed_rows,
    rows_all,
    hidden,
    oc_send,
    oc_recv,
    ox_send,
    ox_recv,
    oz_send,
    oz_recv,
    eo,
    eo_recv,
    w_sem,
    send_sem,
    recv_sem,
):
    y = lax.axis_index("ctx")
    e = lax.axis_index("exp")
    z, x, k = e // 4, (e // 2) % 2, e % 2
    width = mixed_out.shape[1]
    half = width // 2
    cols = half // PROJ_PARTS
    ff = hidden.shape[3]
    ff_cols = ff // FF_PARTS
    out_half = width // 4
    out_cols = out_half // OUT_PARTS
    tokens = queries.shape[0]

    def device(yy, zz, xx, kk):
        return (yy, zz * 4 + xx * 2 + kk)

    zs = (z, z + 1 - 2 * (z % 2), (z + 2) % 4, 3 - z)
    other_core = device(y, z, x, 1 - k)
    x_next = device(y, z, 1 - x, k)
    y_next = device(1 - y, z, x, k)
    partners = [other_core, x_next]
    for dy in range(2):
        for dz in range(4):
            if dy or dz:
                partners.append(device((y + dy) % 2, (z + dz) % 4, x, k))

    weight_copies = {}

    def fetch(name, src, dst):
        copy = pltpu.make_async_copy(src, dst, w_sem.at[len(weight_copies)])
        weight_copies[name] = copy
        copy.start()

    fetch("wo", wo_hbm, wo)

    barrier = pltpu.get_barrier_semaphore()
    for partner in partners:
        pl.semaphore_signal(barrier, inc=1, device_id=partner, device_id_type=pl.DeviceIdType.MESH)

    kvh = e * (queries.shape[1] // HEAD_WIDTH) // (QUERY_HEAD_COUNT // KEY_VALUE_HEADS)
    kv_cols = pl.ds(pl.multiple_of(kvh * HEAD_WIDTH, HEAD_WIDTH), HEAD_WIDTH)
    kv[y, 0] = keys[:, kv_cols]
    kv[y, 1] = values[:, kv_cols]
    res[k] = residual[...].astype(F32)
    lanes = lax.broadcasted_iota(jnp.int32, (expert_ids.shape[0], EXTRA), 1) % 64
    gate_rows = jnp.zeros(lanes.shape, F32)
    for slot in range(expert_ids.shape[1]):
        gate_rows += jnp.where(
            expert_ids[:, slot : slot + 1] == lanes, expert_gates[:, slot : slot + 1], 0.0
        )
    table[k] = gate_rows

    pl.semaphore_wait(barrier, len(partners))

    sent = []

    def send(src, dst, to):
        number = len(sent)
        copy = pltpu.make_async_remote_copy(
            src_ref=src,
            dst_ref=dst,
            send_sem=send_sem.at[number],
            recv_sem=recv_sem.at[number],
            device_id=to,
            device_id_type=pl.DeviceIdType.MESH,
        )
        copy.start()
        sent.append(copy)
        return copy

    kv_copy = send(kv.at[y], kv.at[y], y_next)
    res_copy = send(res.at[k], res.at[k], other_core)
    table_copy = send(table.at[k], table.at[k], other_core)

    kv_copy.wait_recv()
    key_all = kv[:, 0].reshape(2 * tokens, HEAD_WIDTH)
    value_all = kv[:, 1].reshape(2 * tokens, HEAD_WIDTH)
    shape = (tokens, 2 * tokens)
    allowed = lax.broadcasted_iota(jnp.int32, shape, 1) <= y * tokens + lax.broadcasted_iota(
        jnp.int32, shape, 0
    )
    scale = 1.0 / HEAD_WIDTH**0.5
    for head in range(queries.shape[1] // HEAD_WIDTH):
        span = slice(head * HEAD_WIDTH, (head + 1) * HEAD_WIDTH)
        scores = (
            lax.dot_general(
                queries[:, span], key_all, (((1,), (1,)), ((), ())), preferred_element_type=F32
            )
            * scale
        )
        scores = jnp.where(allowed, scores, neg_large)
        weights = jnp.where(
            allowed, jnp.exp(scores - jnp.max(scores, axis=1, keepdims=True)), 0.0
        )
        total = jnp.sum(weights, axis=1, keepdims=True)
        numer = jnp.dot(weights.astype(BF), value_all, preferred_element_type=F32)
        heads[:, span] = (numer / total).astype(BF)

    def columns(which, part, span, size):
        return pl.ds(pl.multiple_of(which * span + part * size, size), size)

    weight_copies["wo"].wait()
    to_core = []
    for part in range(PROJ_PARTS):
        piece = jnp.dot(
            heads[...], wo[:, columns(1 - k, part, half, cols)], preferred_element_type=F32
        )
        pc_send[part] = piece.astype(BF)
        to_core.append(send(pc_send.at[part], pc_recv.at[part], other_core))
    fetch("wg", wg_hbm.at[0], wg)
    to_x = []
    for part in range(PROJ_PARTS):
        piece = jnp.dot(
            heads[...], wo[:, columns(k, part, half, cols)], preferred_element_type=F32
        )
        to_core[part].wait_recv()
        piece = (piece + pc_recv[part].astype(F32)).astype(BF)
        for chip in range(tokens // ROWS):
            px_send[part, chip % 2, chip // 2] = piece[chip * ROWS : (chip + 1) * ROWS]
        to_x.append(send(px_send.at[part, 1 - x], px_recv.at[part], x_next))
    fetch("wu", wu_hbm.at[0], wu)
    to_z = []
    for part in range(PROJ_PARTS):
        to_x[part].wait_recv()
        pz_send[part] = (px_send[part, x].astype(F32) + px_recv[part].astype(F32)).astype(BF)
        for dz in range(1, 4):
            zz = (z + dz) % 4
            to_z.append(
                send(pz_send.at[part, zz], pz_recv.at[part, dz - 1], device(y, zz, x, k))
            )
    fetch("wd", wd_hbm.at[0], wd)
    back = []
    for part in range(PROJ_PARTS):
        piece = pz_send[part, z].astype(F32)
        for dz in range(1, 4):
            to_z[part * 3 + dz - 1].wait_recv()
            piece += pz_recv[part, dz - 1].astype(F32)
        place = columns(k, part, half, cols)
        proj[:, place] = piece
        back.append(send(proj.at[:, place], proj.at[:, place], other_core))

    res_copy.wait_recv()
    table_copy.wait_recv()
    for copy in back:
        copy.wait_recv()
    stream = (proj[...] + res[...].reshape(ROWS, width)).astype(BF).astype(F32)
    mean_sq = jnp.mean(stream * stream, axis=1, keepdims=True)
    normed = (stream * lax.rsqrt(mean_sq + eps_norm) * norm_gain[...]).astype(BF)
    gates = table[...].reshape(ROWS, EXTRA)
    gate_high = gates.astype(BF).astype(F32)
    gate_lane = lax.broadcasted_iota(jnp.int32, gates.shape, 1)
    gates = jnp.where(gate_lane < 64, gate_high, gates - gate_high).astype(BF)

    def block(xx, yy, zz):
        return ((zz // 2) * 4 + xx * 2 + yy) * 2 + zz % 2

    own = block(x, y, z)
    for side in range(2):
        rows_all[side, own, :, :half] = normed[:, side * half : (side + 1) * half]
        rows_all[side, own, :, half:] = gates

    def pass_on(number, to):
        place = rows_all.at[k, number]
        return send(place, place, to)

    y1, x1 = y + k * (1 - 2 * y), x + (1 - k) * (1 - 2 * x)
    y2, x2 = y + (1 - k) * (1 - 2 * y), x + k * (1 - 2 * x)
    first_to, second_to = device(y1, z, x1, k), device(y2, z, x2, k)
    along_z = [pass_on(own, device(y, zs[1], x, k))]
    first, second, second_far = {}, {}, {}
    cross = [[], []]
    first[0] = pass_on(own, first_to)
    second[0] = pass_on(own, second_to)
    along_z += [pass_on(own, device(y, zz, x, k)) for zz in zs[2:]]
    mixed_rows[...] = stream.reshape(2, ROWS // 2, width)
    mixed_out[...] = mixed_rows[k].astype(BF)

    def take_z(i):
        along_z[i - 1].wait_recv()
        number = block(x, y, zs[i])
        first[i] = pass_on(number, first_to)
        second[i] = pass_on(number, second_to)
        cross[i // 2].append(pass_on(number, other_core))

    def take_first(i):
        first[i].wait_recv()
        number = block(x1, y1, zs[i])
        second_far[i] = pass_on(number, second_to)
        cross[i // 2].append(pass_on(number, other_core))

    def take_second(i):
        second[i].wait_recv()
        cross[i // 2].append(pass_on(block(x2, y2, zs[i]), other_core))

    def take_far(i):
        second_far[i].wait_recv()
        cross[i // 2].append(pass_on(block(1 - x, 1 - y, zs[i]), other_core))

    chunk_tokens = tokens
    chunk_blocks = chunk_tokens // ROWS
    across = [[], []]

    def chunk_rows(chunk):
        pair = z // 2 + chunk * (1 - 2 * (z // 2))
        return pl.ds(pair * chunk_blocks, chunk_blocks)

    def expert_up(chunk, part):
        span = slice(part * ff_cols, (part + 1) * ff_cols)
        gate = jnp.zeros((chunk_tokens, ff_cols), F32)
        upper = jnp.zeros((chunk_tokens, ff_cols), F32)
        for side in range(2):
            rows = rows_all[side, chunk_rows(chunk), :, :half].reshape(chunk_tokens, half)
            depth = slice(side * half, (side + 1) * half)
            gate += jnp.dot(rows, wg[depth, span], preferred_element_type=F32)
            upper += jnp.dot(rows, wu[depth, span], preferred_element_type=F32)
        hidden[chunk, y, :, span] = (gate / (1.0 + jnp.exp(-gate)) * upper).astype(BF)
        place = hidden.at[chunk, y, :, span]
        across[chunk].append(send(place, place, y_next))

    take_z(1)
    take_first(0)
    take_second(0)
    take_z(2)
    take_first(1)
    take_second(1)
    take_z(3)
    take_far(0)
    take_far(1)
    weight_copies["wg"].wait()
    weight_copies["wu"].wait()
    for copy in cross[0]:
        copy.wait_recv()
    expert_up(0, 0)
    take_first(2)
    take_second(2)
    for part in range(1, FF_PARTS):
        expert_up(0, part)
        if part == 1:
            take_first(3)
            take_second(3)
    take_far(2)
    take_far(3)
    for copy in cross[1]:
        copy.wait_recv()
    for part in range(FF_PARTS):
        expert_up(1, part)

    shares = []
    for chunk in range(2):
        picked = rows_all[0, chunk_rows(chunk), :, half:].reshape(chunk_tokens, EXTRA).astype(F32)
        picked_lane = lax.broadcasted_iota(jnp.int32, picked.shape, 1) % 64
        shares.append(jnp.sum(jnp.where(picked_lane == e, picked, 0.0), axis=1, keepdims=True))
    weight_copies["wd"].wait()

    def down(chunk, which, part):
        place = columns(which, part, out_half, out_cols)
        result = jnp.dot(hidden[chunk, 0], wd[:ff, place], preferred_element_type=F32)
        result += jnp.dot(hidden[chunk, 1], wd[ff:, place], preferred_element_type=F32)
        return result * shares[chunk]

    to_x, to_z = {}, {}

    def outputs_to_core(chunk):
        for copy in across[chunk]:
            copy.wait_recv()
        to_core = []
        for part in range(OUT_PARTS):
            oc_send[chunk, part] = down(chunk, 1 - k, part).astype(BF)
            to_core.append(send(oc_send.at[chunk, part], oc_recv.at[chunk, part], other_core))
        return to_core

    def outputs_to_x(chunk, to_core):
        for part in range(OUT_PARTS):
            piece = down(chunk, k, part)
            to_core[part].wait_recv()
            piece = (piece + oc_recv[chunk, part].astype(F32)).astype(BF)
            ox_send[chunk, part] = piece.reshape(2, 2, 2, ROWS, out_cols)
            to_x[chunk, part] = send(
                ox_send.at[chunk, part, 1 - x], ox_recv.at[chunk, part], x_next
            )

    def outputs_to_z(chunk):
        for part in range(OUT_PARTS):
            to_x[chunk, part].wait_recv()
            oz_send[chunk, part] = (
                ox_send[chunk, part, x].astype(F32) + ox_recv[chunk, part].astype(F32)
            ).astype(BF)
            for dy in range(2):
                for dz in (2 * chunk, 2 * chunk + 1):
                    if dy or dz:
                        yy = y + dy * (1 - 2 * y)
                        to_z[part, dy, dz] = send(
                            oz_send.at[chunk, part, yy, zs[dz] % 2],
                            oz_recv.at[part, dy * 4 + dz],
                            device(yy, zs[dz], x, k),
                        )

    outputs_to_x(0, outputs_to_core(0))
    to_core = outputs_to_core(1)
    outputs_to_z(0)
    outputs_to_x(1, to_core)
    outputs_to_z(1)
    back = []
    for part in range(OUT_PARTS):
        for dy in range(2):
            piece = None
            for dz in range(4):
                if (part, dy, dz) not in to_z:
                    piece = oz_send[0, part, y, z % 2].astype(F32)
                    continue
                to_z[part, dy, dz].wait_recv()
                came = oz_recv[part, dy * 4 + dz].astype(F32)
                piece = came if piece is None else piece + came
            side = y + dy * (1 - 2 * y)
            place = columns(side * 2 + k, part, out_half, out_cols)
            eo[:, :, place] = piece.reshape(2, ROWS // 2, out_cols)
            back.append(send(eo.at[1 - k, :, place], eo_recv.at[:, place], other_core))
    for part in range(OUT_PARTS):
        for side in range(2):
            place = columns(side * 2 + k, part, out_half, out_cols)
            experts_out[:, place] = eo[k, :, place].astype(BF)
    for copy in back:
        copy.wait_recv()
    for part in range(OUT_PARTS):
        for side in range(2):
            place = columns(side * 2 + 1 - k, part, out_half, out_cols)
            experts_out[:, place] = eo_recv[:, place].astype(BF)
    for copy in sent:
        copy.wait_send()


def hand_over(mixed, experts, mixed_out, experts_out, sems):
    first = pltpu.make_async_copy(mixed, mixed_out, sems.at[0])
    second = pltpu.make_async_copy(experts, experts_out, sems.at[1])
    first.start()
    second.start()
    first.wait()
    second.wait()


def layer_on_device(
    queries,
    keys,
    values,
    residual,
    out_weight,
    norm_gain,
    expert_ids,
    expert_gates,
    w_gate,
    w_up,
    w_down,
):
    tokens, head_cols = queries.shape
    own_rows, width = residual.shape
    ff = w_gate.shape[2]
    half = width // 2
    cols = half // PROJ_PARTS
    out_cols = width // 4 // OUT_PARTS
    all_tokens = 2 * tokens
    vmem = pl.BlockSpec(memory_space=pltpu.VMEM)
    hbm = pl.BlockSpec(memory_space=pl.ANY)
    scratch = [
        pltpu.VMEM(out_weight.shape, BF),
        pltpu.VMEM(w_gate.shape[1:], BF),
        pltpu.VMEM(w_up.shape[1:], BF),
        pltpu.VMEM(w_down.shape[1:], BF),
        pltpu.VMEM((2, 2, tokens, HEAD_WIDTH), BF),
        pltpu.VMEM((2, own_rows, width), F32),
        pltpu.VMEM((2, own_rows, EXTRA), F32),
        pltpu.VMEM((tokens, head_cols), BF),
        pltpu.VMEM((PROJ_PARTS, tokens, cols), BF),
        pltpu.VMEM((PROJ_PARTS, tokens, cols), BF),
        pltpu.VMEM((PROJ_PARTS, 2, 4, ROWS, cols), BF),
        pltpu.VMEM((PROJ_PARTS, 4, ROWS, cols), BF),
        pltpu.VMEM((PROJ_PARTS, 4, ROWS, cols), BF),
        pltpu.VMEM((PROJ_PARTS, 3, ROWS, cols), BF),
        pltpu.VMEM((ROWS, width), F32),
        pltpu.VMEM((2, own_rows, width), F32),
        pltpu.VMEM((2, 16, ROWS, half + EXTRA), BF),
        pltpu.VMEM((2, 2, tokens, ff), BF),
        pltpu.VMEM((2, OUT_PARTS, tokens, out_cols), BF),
        pltpu.VMEM((2, OUT_PARTS, tokens, out_cols), BF),
        pltpu.VMEM((2, OUT_PARTS, 2, 2, 2, ROWS, out_cols), BF),
        pltpu.VMEM((2, OUT_PARTS, 2, 2, ROWS, out_cols), BF),
        pltpu.VMEM((2, OUT_PARTS, 2, 2, ROWS, out_cols), BF),
        pltpu.VMEM((OUT_PARTS, 8, ROWS, out_cols), BF),
        pltpu.VMEM((2, own_rows, width), F32),
        pltpu.VMEM((own_rows, width), F32),
        pltpu.SemaphoreType.DMA((16,)),
        pltpu.SemaphoreType.DMA((96,)),
        pltpu.SemaphoreType.DMA((96,)),
    ]
    flops = 2 * all_tokens * width * ff * 4 + 2 * tokens * head_cols * width
    mixed, experts = pl.pallas_call(
        layer_kernel,
        out_shape=[jax.ShapeDtypeStruct((own_rows, width), BF)] * 2,
        in_specs=[vmem] * 7 + [hbm] * 4,
        out_specs=[vmem] * 2,
        scratch_shapes=scratch,
        compiler_params=pltpu.CompilerParams(
            collective_id=0, has_side_effects=True, vmem_limit_bytes=56 * 2**20
        ),
        cost_estimate=pl.CostEstimate(
            flops=flops, bytes_accessed=24 * 2**20, transcendentals=2**18
        ),
    )(
        queries,
        keys,
        values,
        residual,
        norm_gain.reshape(1, width),
        expert_ids,
        expert_gates,
        out_weight,
        w_gate,
        w_up,
        w_down,
    )
    return tuple(
        pl.pallas_call(
            hand_over,
            out_shape=[jax.ShapeDtypeStruct((own_rows, width), BF)] * 2,
            in_specs=[hbm] * 2,
            out_specs=[hbm] * 2,
            scratch_shapes=[pltpu.SemaphoreType.DMA((2,))],
        )(mixed, experts)
    )


def solution(mesh):
    one_block = mesh.shape["ctx"] == 2 and mesh.shape["exp"] == 16
    return jax.shard_map(
        layer_on_device if one_block else on_device,
        mesh=mesh,
        in_specs=(
            P("ctx", "exp"),
            P("ctx", None),
            P("ctx", None),
            P(("ctx", "exp"), None),
            P("exp", None),
            P(),
            P(("ctx", "exp"), None),
            P(("ctx", "exp"), None),
            P("exp", None, "ctx"),
            P("exp", None, "ctx"),
            P("exp", None, "ctx"),
        ),
        out_specs=(P(("ctx", "exp"), None), P(("ctx", "exp"), None)),
        check_vma=False,
    )
```

```python
import jax
import jax.numpy as jnp
from jax import lax
from jax.experimental import pallas as pl
from jax.experimental.pallas import tpu as pltpu
from jax.sharding import PartitionSpec as P

QUERY_HEAD_COUNT = 64
KEY_VALUE_HEADS = 4
HEAD_WIDTH = 128


neg_large = -1e30
eps_norm = 1e-06


def shifted(value, axis, by):
    size = lax.axis_size(axis)
    pairs = [(i, i + by) for i in range(size) if 0 <= i + by < size]
    return lax.ppermute(value, axis, pairs)


def slot_numbers(expert_ids):
    tok_rows, top_count = expert_ids.shape
    flat_ids = expert_ids.reshape(-1)
    owner_row = jnp.arange(tok_rows * top_count, dtype=jnp.int32) // top_count
    earlier = (flat_ids[:, None] == flat_ids[None, :]) & (owner_row[None, :] < owner_row[:, None])
    return jnp.sum(earlier.astype(jnp.int32), axis=1).reshape(tok_rows, top_count)


def route_hits(expert_ids, slot_ids, expert_count, capacity):
    expert_hit = (
        expert_ids[None, None, :, :]
        == jnp.arange(expert_count, dtype=jnp.int32)[:, None, None, None]
    )
    slot_hit = (
        slot_ids[None, None, :, :] == jnp.arange(capacity, dtype=jnp.int32)[None, :, None, None]
    )
    return expert_hit & slot_hit


def expert_hidden(rows_block, gate_local, up_local):
    gate = jnp.dot(rows_block, gate_local, preferred_element_type=jnp.float32)
    upper = jnp.dot(rows_block, up_local, preferred_element_type=jnp.float32)
    return (jax.nn.silu(gate) * upper).astype(jnp.bfloat16)


def on_device(
    queries,
    keys,
    values,
    residual,
    out_weight,
    norm_gain,
    expert_ids,
    expert_gates,
    w_gate,
    w_up,
    w_down,
):
    tok_query = queries.shape[0]
    device_share = queries.shape[1] // HEAD_WIDTH
    ctx_pos = lax.axis_index("ctx")
    key_value_head = lax.axis_index("exp") * device_share // (QUERY_HEAD_COUNT // KEY_VALUE_HEADS)
    own_keys = lax.dynamic_slice_in_dim(keys, key_value_head * HEAD_WIDTH, HEAD_WIDTH, 1)
    own_values = lax.dynamic_slice_in_dim(values, key_value_head * HEAD_WIDTH, HEAD_WIDTH, 1)
    own_block = jnp.stack([own_keys, own_values])
    query_heads = queries.reshape(tok_query, device_share, HEAD_WIDTH)
    query_start = ctx_pos * tok_query
    query_pos = query_start + jnp.arange(tok_query, dtype=jnp.int32)
    scale = 1.0 / HEAD_WIDTH**0.5
    start_state = (
        jnp.full((device_share, tok_query), neg_large, jnp.float32),
        jnp.zeros((device_share, tok_query), jnp.float32),
        jnp.zeros((device_share, tok_query, HEAD_WIDTH), jnp.float32),
    )

    def attend(state_now, kv_piece, key_start):

        def compute(current):
            running_max, running_sum, weighted = current
            key_pos = key_start + jnp.arange(kv_piece.shape[1], dtype=jnp.int32)
            allowed = key_pos[None, :] <= query_pos[:, None]
            scores = (
                jnp.einsum(
                    "qhd,kd->hqk", query_heads, kv_piece[0], preferred_element_type=jnp.float32
                )
                * scale
            )
            scores = jnp.where(allowed[None], scores, neg_large)
            new_max = jnp.maximum(running_max, jnp.max(scores, axis=2))
            weights_blk = jnp.where(allowed[None], jnp.exp(scores - new_max[:, :, None]), 0.0)
            shrink = jnp.exp(running_max - new_max)
            new_sum = running_sum * shrink + jnp.sum(weights_blk, axis=2)
            added = jnp.einsum(
                "hqk,kd->hqd",
                weights_blk.astype(jnp.bfloat16),
                kv_piece[1],
                preferred_element_type=jnp.float32,
            )
            return (new_max, new_sum, weighted * shrink[:, :, None] + added)

        def unchanged(current):
            return current

        useful = (key_start >= 0) & (key_start <= query_start + tok_query - 1)
        return lax.cond(useful, compute, unchanged, state_now)

    ctx_count = lax.axis_size("ctx")
    state_now = attend(start_state, own_block, query_start)

    def cycle_turn(cycle_step, carried):
        state_cur, moving = carried
        moving = shifted(moving, "ctx", 1)
        source = ctx_pos - cycle_step
        return (attend(state_cur, moving, source * tok_query), moving)

    state_now, _ = lax.fori_loop(1, ctx_count, cycle_turn, (state_now, own_block))
    running_max, running_sum, weighted = state_now
    heads_done = (weighted / running_sum[:, :, None]).astype(jnp.bfloat16)
    heads_done = jnp.transpose(heads_done, (1, 0, 2)).reshape(tok_query, device_share * HEAD_WIDTH)
    tok_rows, top_count = expert_ids.shape
    projected = lax.psum_scatter(
        jnp.dot(heads_done, out_weight, preferred_element_type=jnp.float32).astype(jnp.bfloat16),
        "exp",
        scatter_dimension=0,
        tiled=True,
    ).astype(jnp.float32)
    mixed = (residual.astype(jnp.float32) + projected).astype(jnp.bfloat16)
    stream = mixed.astype(jnp.float32)
    mean_sq = jnp.mean(stream * stream, axis=1, keepdims=True)
    normed = (stream * lax.rsqrt(mean_sq + eps_norm) * norm_gain[None, :]).astype(jnp.bfloat16)
    expert_count = lax.axis_size("exp")
    ctx_count = lax.axis_size("ctx")
    capacity = min(tok_rows, 2 * tok_rows * top_count // expert_count)
    slot_ids = slot_numbers(expert_ids)
    hits = route_hits(expert_ids, slot_ids, expert_count, capacity)
    send_table = jnp.any(hits, axis=3).astype(jnp.bfloat16)
    gate_local = w_gate[0]
    up_local = w_up[0]
    down_local = w_down[0]
    width = normed.shape[1]
    outgoing = jnp.einsum(
        "ecm,md->ecd", send_table, normed, preferred_element_type=jnp.float32
    ).astype(jnp.bfloat16)
    arrived = lax.all_to_all(outgoing, "exp", split_axis=0, concat_axis=0, tiled=True)
    local_rows = arrived.reshape(-1, width)
    hidden = expert_hidden(
        lax.all_gather(local_rows, "ctx", axis=0, tiled=True), gate_local, up_local
    )
    expert_result = jnp.dot(
        lax.all_gather(hidden, "ctx", axis=1, tiled=True),
        down_local,
        preferred_element_type=jnp.float32,
    ).astype(jnp.bfloat16)
    expert_result = expert_result.reshape(ctx_count, expert_count, capacity, down_local.shape[1])
    returned = lax.all_to_all(
        lax.all_to_all(expert_result, "ctx", split_axis=0, concat_axis=3, tiled=True),
        "exp",
        split_axis=1,
        concat_axis=0,
        tiled=True,
    )
    returned = returned.reshape(expert_count, capacity, width)
    mix_table = jnp.sum(jnp.where(hits, expert_gates[None, None, :, :], 0.0), axis=3)
    experts_out = jnp.einsum(
        "ecm,ecd->md", mix_table, returned.astype(jnp.float32), precision=lax.Precision.HIGHEST
    )
    return (mixed, experts_out.astype(jnp.bfloat16))


BF = jnp.bfloat16
F32 = jnp.float32
ROWS = 16
EXTRA = 128
PROJ_PARTS = 8
FF_PARTS = 3
OUT_PARTS = 4


def layer_kernel(
    queries,
    keys,
    values,
    residual,
    norm_gain,
    expert_ids,
    expert_gates,
    wo_hbm,
    wg_hbm,
    wu_hbm,
    wd_hbm,
    results,
    wo,
    wg,
    wu,
    wd,
    kv,
    res,
    table,
    heads,
    pc_send,
    pc_recv,
    px_send,
    px_recv,
    pz_send,
    pz_recv,
    proj,
    mixed_rows,
    rows_all,
    hidden,
    oc_send,
    oc_recv,
    ox_send,
    ox_recv,
    oz_send,
    oz_recv,
    eo,
    eo_recv,
    own_down,
    w_sem,
    send_sem,
    recv_sem,
):
    y = lax.axis_index("ctx")
    e = lax.axis_index("exp")
    z, x, k = e // 4, (e // 2) % 2, e % 2
    width = residual.shape[1]
    half = width // 2
    cols = half // PROJ_PARTS
    ff = hidden.shape[2]
    ff_cols = ff // FF_PARTS
    out_half = width // 4
    out_cols = out_half // OUT_PARTS
    tokens = queries.shape[0]

    def device(yy, zz, xx, kk):
        return (yy, zz * 4 + xx * 2 + kk)

    other_core = device(y, z, x, 1 - k)
    x_next = device(y, z, 1 - x, k)
    y_next = device(1 - y, z, x, k)
    partners = [other_core, x_next]
    for dy in range(2):
        for dz in range(4):
            if dy or dz:
                partners.append(device((y + dy) % 2, (z + dz) % 4, x, k))

    weight_copies = {}

    def fetch(name, src, dst):
        copy = pltpu.make_async_copy(src, dst, w_sem.at[len(weight_copies)])
        weight_copies[name] = copy
        copy.start()

    fetch("wo", wo_hbm, wo)

    barrier = pltpu.get_barrier_semaphore()
    for partner in partners:
        pl.semaphore_signal(barrier, inc=1, device_id=partner, device_id_type=pl.DeviceIdType.MESH)

    kvh = e * (queries.shape[1] // HEAD_WIDTH) // (QUERY_HEAD_COUNT // KEY_VALUE_HEADS)
    kv_cols = pl.ds(pl.multiple_of(kvh * HEAD_WIDTH, HEAD_WIDTH), HEAD_WIDTH)
    kv[y, 0] = keys[:, kv_cols]
    kv[y, 1] = values[:, kv_cols]
    res[k] = residual[...].astype(F32)
    lanes = lax.broadcasted_iota(jnp.int32, (expert_ids.shape[0], EXTRA), 1) % 64
    gate_rows = jnp.zeros(lanes.shape, F32)
    for slot in range(expert_ids.shape[1]):
        gate_rows += jnp.where(
            expert_ids[:, slot : slot + 1] == lanes, expert_gates[:, slot : slot + 1], 0.0
        )
    table[k] = gate_rows

    pl.semaphore_wait(barrier, len(partners))

    sent = []

    def send(src, dst, to):
        number = len(sent)
        copy = pltpu.make_async_remote_copy(
            src_ref=src,
            dst_ref=dst,
            send_sem=send_sem.at[number],
            recv_sem=recv_sem.at[number],
            device_id=to,
            device_id_type=pl.DeviceIdType.MESH,
        )
        copy.start()
        sent.append(copy)
        return copy

    kv_copy = send(kv.at[y], kv.at[y], y_next)
    res_copy = send(res.at[k], res.at[k], other_core)
    table_copy = send(table.at[k], table.at[k], other_core)

    kv_copy.wait_recv()
    key_all = kv[:, 0].reshape(2 * tokens, HEAD_WIDTH)
    value_all = kv[:, 1].reshape(2 * tokens, HEAD_WIDTH)
    shape = (tokens, 2 * tokens)
    allowed = lax.broadcasted_iota(jnp.int32, shape, 1) <= y * tokens + lax.broadcasted_iota(
        jnp.int32, shape, 0
    )
    scale = 1.0 / HEAD_WIDTH**0.5
    for head in range(queries.shape[1] // HEAD_WIDTH):
        span = slice(head * HEAD_WIDTH, (head + 1) * HEAD_WIDTH)
        scores = (
            lax.dot_general(
                queries[:, span], key_all, (((1,), (1,)), ((), ())), preferred_element_type=F32
            )
            * scale
        )
        scores = jnp.where(allowed, scores, neg_large)
        weights = jnp.where(
            allowed, jnp.exp(scores - jnp.max(scores, axis=1, keepdims=True)), 0.0
        )
        total = jnp.sum(weights, axis=1, keepdims=True)
        numer = jnp.dot(weights.astype(BF), value_all, preferred_element_type=F32)
        heads[:, span] = (numer / total).astype(BF)

    def columns(which, part, span, size):
        return pl.ds(pl.multiple_of(which * span + part * size, size), size)

    weight_copies["wo"].wait()
    to_core = []
    for part in range(PROJ_PARTS):
        piece = jnp.dot(
            heads[...], wo[:, columns(1 - k, part, half, cols)], preferred_element_type=F32
        )
        pc_send[part] = piece.astype(BF)
        to_core.append(send(pc_send.at[part], pc_recv.at[part], other_core))
    fetch("wg", wg_hbm.at[0], wg)
    to_x = []
    for part in range(PROJ_PARTS):
        piece = jnp.dot(
            heads[...], wo[:, columns(k, part, half, cols)], preferred_element_type=F32
        )
        to_core[part].wait_recv()
        piece = (piece + pc_recv[part].astype(F32)).astype(BF)
        for chip in range(tokens // ROWS):
            px_send[part, chip % 2, chip // 2] = piece[chip * ROWS : (chip + 1) * ROWS]
        to_x.append(send(px_send.at[part, 1 - x], px_recv.at[part], x_next))
    fetch("wu", wu_hbm.at[0], wu)
    to_z = []
    for part in range(PROJ_PARTS):
        to_x[part].wait_recv()
        pz_send[part] = (px_send[part, x].astype(F32) + px_recv[part].astype(F32)).astype(BF)
        for dz in range(1, 4):
            zz = (z + dz) % 4
            to_z.append(
                send(pz_send.at[part, zz], pz_recv.at[part, dz - 1], device(y, zz, x, k))
            )
    fetch("wd", wd_hbm.at[0], wd)
    back = []
    for part in range(PROJ_PARTS):
        piece = pz_send[part, z].astype(F32)
        for dz in range(1, 4):
            to_z[part * 3 + dz - 1].wait_recv()
            piece += pz_recv[part, dz - 1].astype(F32)
        place = columns(k, part, half, cols)
        proj[:, place] = piece
        back.append(send(proj.at[:, place], proj.at[:, place], other_core))

    res_copy.wait_recv()
    table_copy.wait_recv()
    for copy in back:
        copy.wait_recv()
    stream = (proj[...] + res[...].reshape(ROWS, width)).astype(BF).astype(F32)
    mean_sq = jnp.mean(stream * stream, axis=1, keepdims=True)
    normed = (stream * lax.rsqrt(mean_sq + eps_norm) * norm_gain[...]).astype(BF)
    gates = table[...].reshape(ROWS, EXTRA)
    gate_high = gates.astype(BF).astype(F32)
    gate_lane = lax.broadcasted_iota(jnp.int32, gates.shape, 1)
    gates = jnp.where(gate_lane < 64, gate_high, gates - gate_high).astype(BF)

    def block(xx, yy, zz):
        return (xx * 2 + yy) * 4 + zz

    own = block(x, y, z)
    for side in range(2):
        rows_all[side, own, :, :half] = normed[:, side * half : (side + 1) * half]
        rows_all[side, own, :, half:] = gates

    def pass_on(number, to):
        place = rows_all.at[k, number]
        return send(place, place, to)

    y1, x1 = y + k * (1 - 2 * y), x + (1 - k) * (1 - 2 * x)
    y2, x2 = y + (1 - k) * (1 - 2 * y), x + k * (1 - 2 * x)
    first_to, second_to = device(y1, z, x1, k), device(y2, z, x2, k)
    along_z = [
        pass_on(own, device(y, (z + dz) % 4, x, k)) for dz in range(1, 4)
    ]
    first, second, second_far, cross = [], [], [], []
    first.append(pass_on(own, first_to))
    second.append(pass_on(own, second_to))
    mixed_rows[...] = stream.reshape(2, ROWS // 2, width)
    results[0] = mixed_rows[k].astype(BF)
    for i in range(1, 4):
        along_z[i - 1].wait_recv()
        number = block(x, y, (z + 4 - i) % 4)
        first.append(pass_on(number, first_to))
        second.append(pass_on(number, second_to))
        cross.append(pass_on(number, other_core))
    for i in range(4):
        first[i].wait_recv()
        number = block(x1, y1, (z + 4 - i) % 4)
        second_far.append(pass_on(number, second_to))
        cross.append(pass_on(number, other_core))
    for i in range(4):
        second[i].wait_recv()
        cross.append(pass_on(block(x2, y2, (z + 4 - i) % 4), other_core))
    for i in range(4):
        second_far[i].wait_recv()
        cross.append(pass_on(block(1 - x, 1 - y, (z + 4 - i) % 4), other_core))
    weight_copies["wg"].wait()
    weight_copies["wu"].wait()
    for copy in cross:
        copy.wait_recv()

    all_tokens = rows_all.shape[1] * ROWS
    across = []
    for part in range(FF_PARTS):
        span = slice(part * ff_cols, (part + 1) * ff_cols)
        gate = jnp.zeros((all_tokens, ff_cols), F32)
        upper = jnp.zeros((all_tokens, ff_cols), F32)
        for side in range(2):
            rows = rows_all[side, :, :, :half].reshape(all_tokens, half)
            depth = slice(side * half, (side + 1) * half)
            gate += jnp.dot(rows, wg[depth, span], preferred_element_type=F32)
            upper += jnp.dot(rows, wu[depth, span], preferred_element_type=F32)
        hidden[y, :, span] = (gate / (1.0 + jnp.exp(-gate)) * upper).astype(BF)
        place = hidden.at[y, :, span]
        across.append(send(place, place, y_next))
    picked = rows_all[0, :, :, half:].reshape(all_tokens, EXTRA).astype(F32)
    picked_lane = lax.broadcasted_iota(jnp.int32, picked.shape, 1) % 64
    share = jnp.sum(jnp.where(picked_lane == e, picked, 0.0), axis=1, keepdims=True)
    weight_copies["wd"].wait()
    own_depth = pl.ds(pl.multiple_of(y * ff, ff), ff)
    far_depth = pl.ds(pl.multiple_of((1 - y) * ff, ff), ff)
    for which in range(2 * OUT_PARTS):
        span = slice(which * out_cols, (which + 1) * out_cols)
        own_down[which] = jnp.dot(
            hidden[y], wd[own_depth, span], preferred_element_type=F32
        )
    for copy in across:
        copy.wait_recv()

    def down(which, part):
        place = columns(which, part, out_half, out_cols)
        result = jnp.dot(hidden[1 - y], wd[far_depth, place], preferred_element_type=F32)
        return (result + own_down[which * OUT_PARTS + part]) * share

    to_core, to_x, to_z = [], [], []
    for part in range(OUT_PARTS):
        oc_send[part] = down(1 - k, part).astype(BF)
        to_core.append(send(oc_send.at[part], oc_recv.at[part], other_core))
    for part in range(OUT_PARTS):
        piece = down(k, part)
        to_core[part].wait_recv()
        piece = (piece + oc_recv[part].astype(F32)).astype(BF)
        ox_send[part] = piece.reshape(2, 8, ROWS, out_cols)
        to_x.append(send(ox_send.at[part, 1 - x], ox_recv.at[part], x_next))
    for part in range(OUT_PARTS):
        to_x[part].wait_recv()
        oz_send[part] = (ox_send[part, x].astype(F32) + ox_recv[part].astype(F32)).astype(BF)
        for dy in range(2):
            for dz in range(4):
                if dy or dz:
                    yy, zz = (y + dy) % 2, (z + dz) % 4
                    to_z.append(
                        send(
                            oz_send.at[part, yy * 4 + zz],
                            oz_recv.at[part, dy * 4 + dz],
                            device(yy, zz, x, k),
                        )
                    )
                else:
                    to_z.append(None)
    back = []
    for part in range(OUT_PARTS):
        for dy in range(2):
            piece = None
            for dz in range(4):
                copy = to_z[part * 8 + dy * 4 + dz]
                if copy is None:
                    piece = oz_send[part, y * 4 + z].astype(F32)
                    continue
                copy.wait_recv()
                came = oz_recv[part, dy * 4 + dz].astype(F32)
                piece = came if piece is None else piece + came
            side = y + dy * (1 - 2 * y)
            place = columns(side * 2 + k, part, out_half, out_cols)
            eo[:, :, place] = piece.reshape(2, ROWS // 2, out_cols)
            back.append(send(eo.at[1 - k, :, place], eo_recv.at[:, place], other_core))
    for part in range(OUT_PARTS):
        for side in range(2):
            place = columns(side * 2 + k, part, out_half, out_cols)
            results[1, :, place] = eo[k, :, place].astype(BF)
    for copy in back:
        copy.wait_recv()
    for part in range(OUT_PARTS):
        for side in range(2):
            place = columns(side * 2 + 1 - k, part, out_half, out_cols)
            results[1, :, place] = eo_recv[:, place].astype(BF)
    for copy in sent:
        copy.wait_send()


def layer_on_device(
    queries,
    keys,
    values,
    residual,
    out_weight,
    norm_gain,
    expert_ids,
    expert_gates,
    w_gate,
    w_up,
    w_down,
):
    tokens, head_cols = queries.shape
    own_rows, width = residual.shape
    ff = w_gate.shape[2]
    half = width // 2
    cols = half // PROJ_PARTS
    out_cols = width // 4 // OUT_PARTS
    all_tokens = 2 * tokens
    vmem = pl.BlockSpec(memory_space=pltpu.VMEM)
    hbm = pl.BlockSpec(memory_space=pl.ANY)
    scratch = [
        pltpu.VMEM(out_weight.shape, BF),
        pltpu.VMEM(w_gate.shape[1:], BF),
        pltpu.VMEM(w_up.shape[1:], BF),
        pltpu.VMEM(w_down.shape[1:], BF),
        pltpu.VMEM((2, 2, tokens, HEAD_WIDTH), BF),
        pltpu.VMEM((2, own_rows, width), F32),
        pltpu.VMEM((2, own_rows, EXTRA), F32),
        pltpu.VMEM((tokens, head_cols), BF),
        pltpu.VMEM((PROJ_PARTS, tokens, cols), BF),
        pltpu.VMEM((PROJ_PARTS, tokens, cols), BF),
        pltpu.VMEM((PROJ_PARTS, 2, 4, ROWS, cols), BF),
        pltpu.VMEM((PROJ_PARTS, 4, ROWS, cols), BF),
        pltpu.VMEM((PROJ_PARTS, 4, ROWS, cols), BF),
        pltpu.VMEM((PROJ_PARTS, 3, ROWS, cols), BF),
        pltpu.VMEM((ROWS, width), F32),
        pltpu.VMEM((2, own_rows, width), F32),
        pltpu.VMEM((2, 16, ROWS, half + EXTRA), BF),
        pltpu.VMEM((2, all_tokens, ff), BF),
        pltpu.VMEM((OUT_PARTS, all_tokens, out_cols), BF),
        pltpu.VMEM((OUT_PARTS, all_tokens, out_cols), BF),
        pltpu.VMEM((OUT_PARTS, 2, 8, ROWS, out_cols), BF),
        pltpu.VMEM((OUT_PARTS, 8, ROWS, out_cols), BF),
        pltpu.VMEM((OUT_PARTS, 8, ROWS, out_cols), BF),
        pltpu.VMEM((OUT_PARTS, 8, ROWS, out_cols), BF),
        pltpu.VMEM((2, own_rows, width), F32),
        pltpu.VMEM((own_rows, width), F32),
        pltpu.VMEM((2 * OUT_PARTS, all_tokens, out_cols), F32),
        pltpu.SemaphoreType.DMA((16,)),
        pltpu.SemaphoreType.DMA((136,)),
        pltpu.SemaphoreType.DMA((136,)),
    ]
    flops = 2 * all_tokens * width * ff * 4 + 2 * tokens * head_cols * width
    results = pl.pallas_call(
        layer_kernel,
        out_shape=jax.ShapeDtypeStruct((2, own_rows, width), BF),
        in_specs=[vmem] * 7 + [hbm] * 4,
        out_specs=vmem,
        scratch_shapes=scratch,
        compiler_params=pltpu.CompilerParams(
            collective_id=0, has_side_effects=True, vmem_limit_bytes=56 * 2**20
        ),
        cost_estimate=pl.CostEstimate(
            flops=flops, bytes_accessed=24 * 2**20, transcendentals=2**18
        ),
    )(
        queries,
        keys,
        values,
        residual,
        norm_gain.reshape(1, width),
        expert_ids,
        expert_gates,
        out_weight,
        w_gate,
        w_up,
        w_down,
    )
    return results[0], results[1]


def solution(mesh):
    one_block = mesh.shape["ctx"] == 2 and mesh.shape["exp"] == 16
    return jax.shard_map(
        layer_on_device if one_block else on_device,
        mesh=mesh,
        in_specs=(
            P("ctx", "exp"),
            P("ctx", None),
            P("ctx", None),
            P(("ctx", "exp"), None),
            P("exp", None),
            P(),
            P(("ctx", "exp"), None),
            P(("ctx", "exp"), None),
            P("exp", None, "ctx"),
            P("exp", None, "ctx"),
            P("exp", None, "ctx"),
        ),
        out_specs=(P(("ctx", "exp"), None), P(("ctx", "exp"), None)),
        check_vma=False,
    )
```

```python
import jax
import jax.numpy as jnp
from jax import lax
from jax.experimental import pallas as pl
from jax.experimental.pallas import tpu as pltpu
from jax.sharding import PartitionSpec as P

QUERY_HEAD_COUNT = 64
KEY_VALUE_HEADS = 4
HEAD_WIDTH = 128


neg_large = -1e30
eps_norm = 1e-06


def shifted(value, axis, by):
    size = lax.axis_size(axis)
    pairs = [(i, i + by) for i in range(size) if 0 <= i + by < size]
    return lax.ppermute(value, axis, pairs)


def slot_numbers(expert_ids):
    tok_rows, top_count = expert_ids.shape
    flat_ids = expert_ids.reshape(-1)
    owner_row = jnp.arange(tok_rows * top_count, dtype=jnp.int32) // top_count
    earlier = (flat_ids[:, None] == flat_ids[None, :]) & (owner_row[None, :] < owner_row[:, None])
    return jnp.sum(earlier.astype(jnp.int32), axis=1).reshape(tok_rows, top_count)


def route_hits(expert_ids, slot_ids, expert_count, capacity):
    expert_hit = (
        expert_ids[None, None, :, :]
        == jnp.arange(expert_count, dtype=jnp.int32)[:, None, None, None]
    )
    slot_hit = (
        slot_ids[None, None, :, :] == jnp.arange(capacity, dtype=jnp.int32)[None, :, None, None]
    )
    return expert_hit & slot_hit


def expert_hidden(rows_block, gate_local, up_local):
    gate = jnp.dot(rows_block, gate_local, preferred_element_type=jnp.float32)
    upper = jnp.dot(rows_block, up_local, preferred_element_type=jnp.float32)
    return (jax.nn.silu(gate) * upper).astype(jnp.bfloat16)


def on_device(
    queries,
    keys,
    values,
    residual,
    out_weight,
    norm_gain,
    expert_ids,
    expert_gates,
    w_gate,
    w_up,
    w_down,
):
    tok_query = queries.shape[0]
    device_share = queries.shape[1] // HEAD_WIDTH
    ctx_pos = lax.axis_index("ctx")
    key_value_head = lax.axis_index("exp") * device_share // (QUERY_HEAD_COUNT // KEY_VALUE_HEADS)
    own_keys = lax.dynamic_slice_in_dim(keys, key_value_head * HEAD_WIDTH, HEAD_WIDTH, 1)
    own_values = lax.dynamic_slice_in_dim(values, key_value_head * HEAD_WIDTH, HEAD_WIDTH, 1)
    own_block = jnp.stack([own_keys, own_values])
    query_heads = queries.reshape(tok_query, device_share, HEAD_WIDTH)
    query_start = ctx_pos * tok_query
    query_pos = query_start + jnp.arange(tok_query, dtype=jnp.int32)
    scale = 1.0 / HEAD_WIDTH**0.5
    start_state = (
        jnp.full((device_share, tok_query), neg_large, jnp.float32),
        jnp.zeros((device_share, tok_query), jnp.float32),
        jnp.zeros((device_share, tok_query, HEAD_WIDTH), jnp.float32),
    )

    def attend(state_now, kv_piece, key_start):

        def compute(current):
            running_max, running_sum, weighted = current
            key_pos = key_start + jnp.arange(kv_piece.shape[1], dtype=jnp.int32)
            allowed = key_pos[None, :] <= query_pos[:, None]
            scores = (
                jnp.einsum(
                    "qhd,kd->hqk", query_heads, kv_piece[0], preferred_element_type=jnp.float32
                )
                * scale
            )
            scores = jnp.where(allowed[None], scores, neg_large)
            new_max = jnp.maximum(running_max, jnp.max(scores, axis=2))
            weights_blk = jnp.where(allowed[None], jnp.exp(scores - new_max[:, :, None]), 0.0)
            shrink = jnp.exp(running_max - new_max)
            new_sum = running_sum * shrink + jnp.sum(weights_blk, axis=2)
            added = jnp.einsum(
                "hqk,kd->hqd",
                weights_blk.astype(jnp.bfloat16),
                kv_piece[1],
                preferred_element_type=jnp.float32,
            )
            return (new_max, new_sum, weighted * shrink[:, :, None] + added)

        def unchanged(current):
            return current

        useful = (key_start >= 0) & (key_start <= query_start + tok_query - 1)
        return lax.cond(useful, compute, unchanged, state_now)

    ctx_count = lax.axis_size("ctx")
    state_now = attend(start_state, own_block, query_start)

    def cycle_turn(cycle_step, carried):
        state_cur, moving = carried
        moving = shifted(moving, "ctx", 1)
        source = ctx_pos - cycle_step
        return (attend(state_cur, moving, source * tok_query), moving)

    state_now, _ = lax.fori_loop(1, ctx_count, cycle_turn, (state_now, own_block))
    running_max, running_sum, weighted = state_now
    heads_done = (weighted / running_sum[:, :, None]).astype(jnp.bfloat16)
    heads_done = jnp.transpose(heads_done, (1, 0, 2)).reshape(tok_query, device_share * HEAD_WIDTH)
    tok_rows, top_count = expert_ids.shape
    projected = lax.psum_scatter(
        jnp.dot(heads_done, out_weight, preferred_element_type=jnp.float32).astype(jnp.bfloat16),
        "exp",
        scatter_dimension=0,
        tiled=True,
    ).astype(jnp.float32)
    mixed = (residual.astype(jnp.float32) + projected).astype(jnp.bfloat16)
    stream = mixed.astype(jnp.float32)
    mean_sq = jnp.mean(stream * stream, axis=1, keepdims=True)
    normed = (stream * lax.rsqrt(mean_sq + eps_norm) * norm_gain[None, :]).astype(jnp.bfloat16)
    expert_count = lax.axis_size("exp")
    ctx_count = lax.axis_size("ctx")
    capacity = min(tok_rows, 2 * tok_rows * top_count // expert_count)
    slot_ids = slot_numbers(expert_ids)
    hits = route_hits(expert_ids, slot_ids, expert_count, capacity)
    send_table = jnp.any(hits, axis=3).astype(jnp.bfloat16)
    gate_local = w_gate[0]
    up_local = w_up[0]
    down_local = w_down[0]
    width = normed.shape[1]
    outgoing = jnp.einsum(
        "ecm,md->ecd", send_table, normed, preferred_element_type=jnp.float32
    ).astype(jnp.bfloat16)
    arrived = lax.all_to_all(outgoing, "exp", split_axis=0, concat_axis=0, tiled=True)
    local_rows = arrived.reshape(-1, width)
    hidden = expert_hidden(
        lax.all_gather(local_rows, "ctx", axis=0, tiled=True), gate_local, up_local
    )
    expert_result = jnp.dot(
        lax.all_gather(hidden, "ctx", axis=1, tiled=True),
        down_local,
        preferred_element_type=jnp.float32,
    ).astype(jnp.bfloat16)
    expert_result = expert_result.reshape(ctx_count, expert_count, capacity, down_local.shape[1])
    returned = lax.all_to_all(
        lax.all_to_all(expert_result, "ctx", split_axis=0, concat_axis=3, tiled=True),
        "exp",
        split_axis=1,
        concat_axis=0,
        tiled=True,
    )
    returned = returned.reshape(expert_count, capacity, width)
    mix_table = jnp.sum(jnp.where(hits, expert_gates[None, None, :, :], 0.0), axis=3)
    experts_out = jnp.einsum(
        "ecm,ecd->md", mix_table, returned.astype(jnp.float32), precision=lax.Precision.HIGHEST
    )
    return (mixed, experts_out.astype(jnp.bfloat16))


BF = jnp.bfloat16
F32 = jnp.float32
ROWS = 16
EXTRA = 128
PROJ_PARTS = 2
FF_PARTS = 3
OUT_PARTS = 2


def layer_kernel(
    queries,
    keys,
    values,
    residual,
    norm_gain,
    expert_ids,
    expert_gates,
    wo_hbm,
    wg_hbm,
    wu_hbm,
    wd_hbm,
    results,
    wo,
    wg,
    wu,
    wd,
    kv,
    res,
    table,
    heads,
    pc_send,
    pc_recv,
    px_send,
    px_recv,
    pz_send,
    pz_recv,
    proj,
    mixed_rows,
    rows_all,
    hidden,
    oc_send,
    oc_recv,
    ox_send,
    ox_recv,
    oz_send,
    oz_recv,
    eo,
    eo_recv,
    own_down,
    w_sem,
    send_sem,
    recv_sem,
):
    y = lax.axis_index("ctx")
    e = lax.axis_index("exp")
    z, x, k = e // 4, (e // 2) % 2, e % 2
    width = residual.shape[1]
    half = width // 2
    cols = half // PROJ_PARTS
    ff = hidden.shape[2]
    ff_cols = ff // FF_PARTS
    out_half = width // 4
    out_cols = out_half // OUT_PARTS
    tokens = queries.shape[0]

    def device(yy, zz, xx, kk):
        return (yy, zz * 4 + xx * 2 + kk)

    other_core = device(y, z, x, 1 - k)
    x_next = device(y, z, 1 - x, k)
    y_next = device(1 - y, z, x, k)
    partners = [other_core, x_next]
    for dy in range(2):
        for dz in range(4):
            if dy or dz:
                partners.append(device((y + dy) % 2, (z + dz) % 4, x, k))

    weight_copies = {}

    def fetch(name, src, dst):
        copy = pltpu.make_async_copy(src, dst, w_sem.at[len(weight_copies)])
        weight_copies[name] = copy
        copy.start()

    fetch("wo", wo_hbm, wo)

    barrier = pltpu.get_barrier_semaphore()
    for partner in partners:
        pl.semaphore_signal(barrier, inc=1, device_id=partner, device_id_type=pl.DeviceIdType.MESH)

    kvh = e * (queries.shape[1] // HEAD_WIDTH) // (QUERY_HEAD_COUNT // KEY_VALUE_HEADS)
    kv_cols = pl.ds(pl.multiple_of(kvh * HEAD_WIDTH, HEAD_WIDTH), HEAD_WIDTH)
    kv[y, 0] = keys[:, kv_cols]
    kv[y, 1] = values[:, kv_cols]
    res[k] = residual[...].astype(F32)
    lanes = lax.broadcasted_iota(jnp.int32, (expert_ids.shape[0], EXTRA), 1) % 64
    gate_rows = jnp.zeros(lanes.shape, F32)
    for slot in range(expert_ids.shape[1]):
        gate_rows += jnp.where(
            expert_ids[:, slot : slot + 1] == lanes, expert_gates[:, slot : slot + 1], 0.0
        )
    table[k] = gate_rows

    pl.semaphore_wait(barrier, len(partners))

    sent = []

    def send(src, dst, to):
        number = len(sent)
        copy = pltpu.make_async_remote_copy(
            src_ref=src,
            dst_ref=dst,
            send_sem=send_sem.at[number],
            recv_sem=recv_sem.at[number],
            device_id=to,
            device_id_type=pl.DeviceIdType.MESH,
        )
        copy.start()
        sent.append(copy)
        return copy

    kv_copy = send(kv.at[y], kv.at[y], y_next)
    res_copy = send(res.at[k], res.at[k], other_core)
    table_copy = send(table.at[k], table.at[k], other_core)

    kv_copy.wait_recv()
    key_all = kv[:, 0].reshape(2 * tokens, HEAD_WIDTH)
    value_all = kv[:, 1].reshape(2 * tokens, HEAD_WIDTH)
    shape = (tokens, 2 * tokens)
    allowed = lax.broadcasted_iota(jnp.int32, shape, 1) <= y * tokens + lax.broadcasted_iota(
        jnp.int32, shape, 0
    )
    scale = 1.0 / HEAD_WIDTH**0.5
    for head in range(queries.shape[1] // HEAD_WIDTH):
        span = slice(head * HEAD_WIDTH, (head + 1) * HEAD_WIDTH)
        scores = (
            lax.dot_general(
                queries[:, span], key_all, (((1,), (1,)), ((), ())), preferred_element_type=F32
            )
            * scale
        )
        scores = jnp.where(allowed, scores, neg_large)
        weights = jnp.where(
            allowed, jnp.exp(scores - jnp.max(scores, axis=1, keepdims=True)), 0.0
        )
        total = jnp.sum(weights, axis=1, keepdims=True)
        numer = jnp.dot(weights.astype(BF), value_all, preferred_element_type=F32)
        heads[:, span] = (numer / total).astype(BF)

    def columns(which, part, span, size):
        return pl.ds(pl.multiple_of(which * span + part * size, size), size)

    weight_copies["wo"].wait()
    to_core = []
    for part in range(PROJ_PARTS):
        piece = jnp.dot(
            heads[...], wo[:, columns(1 - k, part, half, cols)], preferred_element_type=F32
        )
        pc_send[part] = piece.astype(BF)
        to_core.append(send(pc_send.at[part], pc_recv.at[part], other_core))
    fetch("wg", wg_hbm.at[0], wg)
    to_x = []
    for part in range(PROJ_PARTS):
        piece = jnp.dot(
            heads[...], wo[:, columns(k, part, half, cols)], preferred_element_type=F32
        )
        to_core[part].wait_recv()
        piece = (piece + pc_recv[part].astype(F32)).astype(BF)
        for chip in range(tokens // ROWS):
            px_send[part, chip % 2, chip // 2] = piece[chip * ROWS : (chip + 1) * ROWS]
        to_x.append(send(px_send.at[part, 1 - x], px_recv.at[part], x_next))
    fetch("wu", wu_hbm.at[0], wu)
    to_z = []
    for part in range(PROJ_PARTS):
        to_x[part].wait_recv()
        pz_send[part] = (px_send[part, x].astype(F32) + px_recv[part].astype(F32)).astype(BF)
        for dz in range(1, 4):
            zz = (z + dz) % 4
            to_z.append(
                send(pz_send.at[part, zz], pz_recv.at[part, dz - 1], device(y, zz, x, k))
            )
    fetch("wd", wd_hbm.at[0], wd)
    back = []
    for part in range(PROJ_PARTS):
        piece = pz_send[part, z].astype(F32)
        for dz in range(1, 4):
            to_z[part * 3 + dz - 1].wait_recv()
            piece += pz_recv[part, dz - 1].astype(F32)
        place = columns(k, part, half, cols)
        proj[:, place] = piece
        back.append(send(proj.at[:, place], proj.at[:, place], other_core))

    res_copy.wait_recv()
    table_copy.wait_recv()
    for copy in back:
        copy.wait_recv()
    stream = (proj[...] + res[...].reshape(ROWS, width)).astype(BF).astype(F32)
    mean_sq = jnp.mean(stream * stream, axis=1, keepdims=True)
    normed = (stream * lax.rsqrt(mean_sq + eps_norm) * norm_gain[...]).astype(BF)
    gates = table[...].reshape(ROWS, EXTRA)
    gate_high = gates.astype(BF).astype(F32)
    gate_lane = lax.broadcasted_iota(jnp.int32, gates.shape, 1)
    gates = jnp.where(gate_lane < 64, gate_high, gates - gate_high).astype(BF)

    def block(xx, yy, zz):
        return (xx * 2 + yy) * 4 + zz

    own = block(x, y, z)
    side_rows = jnp.where(k == 0, normed[:, :half], normed[:, half:])
    rows_all[k, own, :, :half] = side_rows
    rows_all[k, own, :, half:] = gates

    def pass_on(number, count, to):
        place = rows_all.at[k, pl.ds(number, count)]
        return send(place, place, to)

    y1, x1 = y + k * (1 - 2 * y), x + (1 - k) * (1 - 2 * x)
    y2, x2 = y + (1 - k) * (1 - 2 * y), x + k * (1 - 2 * x)
    first_to, second_to = device(y1, z, x1, k), device(y2, z, x2, k)
    zs = (z, z + 1 - 2 * (z % 2), (z + 2) % 4, 3 - z)
    along_z = [pass_on(own, 1, device(y, zz, x, k)) for zz in zs[1:]]
    mixed_rows[...] = stream.reshape(2, ROWS // 2, width)
    results[0] = mixed_rows[k].astype(BF)
    pairs = ((z // 2) * 2, 2 - (z // 2) * 2)
    first, second, second_far, cross = [], [], [], []
    for i in range(2):
        if i == 0:
            along_z[0].wait_recv()
        else:
            along_z[1].wait_recv()
            along_z[2].wait_recv()
        number = block(x, y, pairs[i])
        first.append(pass_on(number, 2, first_to))
        second.append(pass_on(number, 2, second_to))
        cross.append(pass_on(number, 2, other_core))
    for i in range(2):
        first[i].wait_recv()
        number = block(x1, y1, pairs[i])
        second_far.append(pass_on(number, 2, second_to))
        cross.append(pass_on(number, 2, other_core))
    for i in range(2):
        second[i].wait_recv()
        cross.append(pass_on(block(x2, y2, pairs[i]), 2, other_core))
    for i in range(2):
        second_far[i].wait_recv()
        cross.append(pass_on(block(1 - x, 1 - y, pairs[i]), 2, other_core))
    weight_copies["wg"].wait()
    weight_copies["wu"].wait()
    for copy in cross:
        copy.wait_recv()

    all_tokens = rows_all.shape[1] * ROWS
    across = []
    for part in range(FF_PARTS):
        span = slice(part * ff_cols, (part + 1) * ff_cols)
        gate = jnp.zeros((all_tokens, ff_cols), F32)
        upper = jnp.zeros((all_tokens, ff_cols), F32)
        for side in range(2):
            rows = rows_all[side, :, :, :half].reshape(all_tokens, half)
            depth = slice(side * half, (side + 1) * half)
            gate += jnp.dot(rows, wg[depth, span], preferred_element_type=F32)
            upper += jnp.dot(rows, wu[depth, span], preferred_element_type=F32)
        hidden[y, :, span] = (gate / (1.0 + jnp.exp(-gate)) * upper).astype(BF)
        place = hidden.at[y, :, span]
        across.append(send(place, place, y_next))
    picked = rows_all[0, :, :, half:].reshape(all_tokens, EXTRA).astype(F32)
    picked_lane = lax.broadcasted_iota(jnp.int32, picked.shape, 1) % 64
    share = jnp.sum(jnp.where(picked_lane == e, picked, 0.0), axis=1, keepdims=True)
    weight_copies["wd"].wait()
    own_depth = pl.ds(pl.multiple_of(y * ff, ff), ff)
    far_depth = pl.ds(pl.multiple_of((1 - y) * ff, ff), ff)
    for which in range(2 * OUT_PARTS):
        span = slice(which * out_cols, (which + 1) * out_cols)
        own_down[which] = jnp.dot(
            hidden[y], wd[own_depth, span], preferred_element_type=F32
        )
    for copy in across:
        copy.wait_recv()

    def down(which, part):
        place = columns(which, part, out_half, out_cols)
        result = jnp.dot(hidden[1 - y], wd[far_depth, place], preferred_element_type=F32)
        return (result + own_down[which * OUT_PARTS + part]) * share

    to_core, to_x, to_z = [], [], []
    for part in range(OUT_PARTS):
        oc_send[part] = down(1 - k, part).astype(BF)
        to_core.append(send(oc_send.at[part], oc_recv.at[part], other_core))
    for part in range(OUT_PARTS):
        piece = down(k, part)
        to_core[part].wait_recv()
        piece = (piece + oc_recv[part].astype(F32)).astype(BF)
        ox_send[part] = piece.reshape(2, 8, ROWS, out_cols)
        to_x.append(send(ox_send.at[part, 1 - x], ox_recv.at[part], x_next))
    for part in range(OUT_PARTS):
        to_x[part].wait_recv()
        oz_send[part] = (ox_send[part, x].astype(F32) + ox_recv[part].astype(F32)).astype(BF)
        for dy in range(2):
            for dz in range(4):
                if dy or dz:
                    yy, zz = (y + dy) % 2, (z + dz) % 4
                    to_z.append(
                        send(
                            oz_send.at[part, yy * 4 + zz],
                            oz_recv.at[part, dy * 4 + dz],
                            device(yy, zz, x, k),
                        )
                    )
                else:
                    to_z.append(None)
    back = []
    for part in range(OUT_PARTS):
        for dy in range(2):
            piece = None
            for dz in range(4):
                copy = to_z[part * 8 + dy * 4 + dz]
                if copy is None:
                    piece = oz_send[part, y * 4 + z].astype(F32)
                    continue
                copy.wait_recv()
                came = oz_recv[part, dy * 4 + dz].astype(F32)
                piece = came if piece is None else piece + came
            side = y + dy * (1 - 2 * y)
            place = columns(side * 2 + k, part, out_half, out_cols)
            eo[:, :, place] = piece.reshape(2, ROWS // 2, out_cols)
            back.append(send(eo.at[1 - k, :, place], eo_recv.at[:, place], other_core))
    for part in range(OUT_PARTS):
        for side in range(2):
            place = columns(side * 2 + k, part, out_half, out_cols)
            results[1, :, place] = eo[k, :, place].astype(BF)
    for copy in back:
        copy.wait_recv()
    for part in range(OUT_PARTS):
        for side in range(2):
            place = columns(side * 2 + 1 - k, part, out_half, out_cols)
            results[1, :, place] = eo_recv[:, place].astype(BF)
    for copy in sent:
        copy.wait_send()


def layer_on_device(
    queries,
    keys,
    values,
    residual,
    out_weight,
    norm_gain,
    expert_ids,
    expert_gates,
    w_gate,
    w_up,
    w_down,
):
    tokens, head_cols = queries.shape
    own_rows, width = residual.shape
    ff = w_gate.shape[2]
    half = width // 2
    cols = half // PROJ_PARTS
    out_cols = width // 4 // OUT_PARTS
    all_tokens = 2 * tokens
    vmem = pl.BlockSpec(memory_space=pltpu.VMEM)
    hbm = pl.BlockSpec(memory_space=pl.ANY)
    scratch = [
        pltpu.VMEM(out_weight.shape, BF),
        pltpu.VMEM(w_gate.shape[1:], BF),
        pltpu.VMEM(w_up.shape[1:], BF),
        pltpu.VMEM(w_down.shape[1:], BF),
        pltpu.VMEM((2, 2, tokens, HEAD_WIDTH), BF),
        pltpu.VMEM((2, own_rows, width), F32),
        pltpu.VMEM((2, own_rows, EXTRA), F32),
        pltpu.VMEM((tokens, head_cols), BF),
        pltpu.VMEM((PROJ_PARTS, tokens, cols), BF),
        pltpu.VMEM((PROJ_PARTS, tokens, cols), BF),
        pltpu.VMEM((PROJ_PARTS, 2, 4, ROWS, cols), BF),
        pltpu.VMEM((PROJ_PARTS, 4, ROWS, cols), BF),
        pltpu.VMEM((PROJ_PARTS, 4, ROWS, cols), BF),
        pltpu.VMEM((PROJ_PARTS, 3, ROWS, cols), BF),
        pltpu.VMEM((ROWS, width), F32),
        pltpu.VMEM((2, own_rows, width), F32),
        pltpu.VMEM((2, 16, ROWS, half + EXTRA), BF),
        pltpu.VMEM((2, all_tokens, ff), BF),
        pltpu.VMEM((OUT_PARTS, all_tokens, out_cols), BF),
        pltpu.VMEM((OUT_PARTS, all_tokens, out_cols), BF),
        pltpu.VMEM((OUT_PARTS, 2, 8, ROWS, out_cols), BF),
        pltpu.VMEM((OUT_PARTS, 8, ROWS, out_cols), BF),
        pltpu.VMEM((OUT_PARTS, 8, ROWS, out_cols), BF),
        pltpu.VMEM((OUT_PARTS, 8, ROWS, out_cols), BF),
        pltpu.VMEM((2, own_rows, width), F32),
        pltpu.VMEM((own_rows, width), F32),
        pltpu.VMEM((2 * OUT_PARTS, all_tokens, out_cols), F32),
        pltpu.SemaphoreType.DMA((16,)),
        pltpu.SemaphoreType.DMA((136,)),
        pltpu.SemaphoreType.DMA((136,)),
    ]
    flops = 2 * all_tokens * width * ff * 4 + 2 * tokens * head_cols * width
    results = pl.pallas_call(
        layer_kernel,
        out_shape=jax.ShapeDtypeStruct((2, own_rows, width), BF),
        in_specs=[vmem] * 7 + [hbm] * 4,
        out_specs=vmem,
        scratch_shapes=scratch,
        compiler_params=pltpu.CompilerParams(
            collective_id=0, has_side_effects=True, vmem_limit_bytes=56 * 2**20
        ),
        cost_estimate=pl.CostEstimate(
            flops=flops, bytes_accessed=24 * 2**20, transcendentals=2**18
        ),
    )(
        queries,
        keys,
        values,
        residual,
        norm_gain.reshape(1, width),
        expert_ids,
        expert_gates,
        out_weight,
        w_gate,
        w_up,
        w_down,
    )
    return results[0], results[1]


def solution(mesh):
    one_block = mesh.shape["ctx"] == 2 and mesh.shape["exp"] == 16
    return jax.shard_map(
        layer_on_device if one_block else on_device,
        mesh=mesh,
        in_specs=(
            P("ctx", "exp"),
            P("ctx", None),
            P("ctx", None),
            P(("ctx", "exp"), None),
            P("exp", None),
            P(),
            P(("ctx", "exp"), None),
            P(("ctx", "exp"), None),
            P("exp", None, "ctx"),
            P("exp", None, "ctx"),
            P("exp", None, "ctx"),
        ),
        out_specs=(P(("ctx", "exp"), None), P(("ctx", "exp"), None)),
        check_vma=False,
    )
```

```python
import jax
import jax.numpy as jnp
from jax import lax
from jax.experimental import pallas as pl
from jax.experimental.pallas import tpu as pltpu
from jax.sharding import PartitionSpec as P

QUERY_HEAD_COUNT = 64
KEY_VALUE_HEADS = 4
HEAD_WIDTH = 128


neg_large = -1e30
eps_norm = 1e-06


def shifted(value, axis, by):
    size = lax.axis_size(axis)
    pairs = [(i, i + by) for i in range(size) if 0 <= i + by < size]
    return lax.ppermute(value, axis, pairs)


def slot_numbers(expert_ids):
    tok_rows, top_count = expert_ids.shape
    flat_ids = expert_ids.reshape(-1)
    owner_row = jnp.arange(tok_rows * top_count, dtype=jnp.int32) // top_count
    earlier = (flat_ids[:, None] == flat_ids[None, :]) & (owner_row[None, :] < owner_row[:, None])
    return jnp.sum(earlier.astype(jnp.int32), axis=1).reshape(tok_rows, top_count)


def route_hits(expert_ids, slot_ids, expert_count, capacity):
    expert_hit = (
        expert_ids[None, None, :, :]
        == jnp.arange(expert_count, dtype=jnp.int32)[:, None, None, None]
    )
    slot_hit = (
        slot_ids[None, None, :, :] == jnp.arange(capacity, dtype=jnp.int32)[None, :, None, None]
    )
    return expert_hit & slot_hit


def expert_hidden(rows_block, gate_local, up_local):
    gate = jnp.dot(rows_block, gate_local, preferred_element_type=jnp.float32)
    upper = jnp.dot(rows_block, up_local, preferred_element_type=jnp.float32)
    return (jax.nn.silu(gate) * upper).astype(jnp.bfloat16)


def on_device(
    queries,
    keys,
    values,
    residual,
    out_weight,
    norm_gain,
    expert_ids,
    expert_gates,
    w_gate,
    w_up,
    w_down,
):
    tok_query = queries.shape[0]
    device_share = queries.shape[1] // HEAD_WIDTH
    ctx_pos = lax.axis_index("ctx")
    key_value_head = lax.axis_index("exp") * device_share // (QUERY_HEAD_COUNT // KEY_VALUE_HEADS)
    own_keys = lax.dynamic_slice_in_dim(keys, key_value_head * HEAD_WIDTH, HEAD_WIDTH, 1)
    own_values = lax.dynamic_slice_in_dim(values, key_value_head * HEAD_WIDTH, HEAD_WIDTH, 1)
    own_block = jnp.stack([own_keys, own_values])
    query_heads = queries.reshape(tok_query, device_share, HEAD_WIDTH)
    query_start = ctx_pos * tok_query
    query_pos = query_start + jnp.arange(tok_query, dtype=jnp.int32)
    scale = 1.0 / HEAD_WIDTH**0.5
    start_state = (
        jnp.full((device_share, tok_query), neg_large, jnp.float32),
        jnp.zeros((device_share, tok_query), jnp.float32),
        jnp.zeros((device_share, tok_query, HEAD_WIDTH), jnp.float32),
    )

    def attend(state_now, kv_piece, key_start):

        def compute(current):
            running_max, running_sum, weighted = current
            key_pos = key_start + jnp.arange(kv_piece.shape[1], dtype=jnp.int32)
            allowed = key_pos[None, :] <= query_pos[:, None]
            scores = (
                jnp.einsum(
                    "qhd,kd->hqk", query_heads, kv_piece[0], preferred_element_type=jnp.float32
                )
                * scale
            )
            scores = jnp.where(allowed[None], scores, neg_large)
            new_max = jnp.maximum(running_max, jnp.max(scores, axis=2))
            weights_blk = jnp.where(allowed[None], jnp.exp(scores - new_max[:, :, None]), 0.0)
            shrink = jnp.exp(running_max - new_max)
            new_sum = running_sum * shrink + jnp.sum(weights_blk, axis=2)
            added = jnp.einsum(
                "hqk,kd->hqd",
                weights_blk.astype(jnp.bfloat16),
                kv_piece[1],
                preferred_element_type=jnp.float32,
            )
            return (new_max, new_sum, weighted * shrink[:, :, None] + added)

        def unchanged(current):
            return current

        useful = (key_start >= 0) & (key_start <= query_start + tok_query - 1)
        return lax.cond(useful, compute, unchanged, state_now)

    ctx_count = lax.axis_size("ctx")
    state_now = attend(start_state, own_block, query_start)

    def cycle_turn(cycle_step, carried):
        state_cur, moving = carried
        moving = shifted(moving, "ctx", 1)
        source = ctx_pos - cycle_step
        return (attend(state_cur, moving, source * tok_query), moving)

    state_now, _ = lax.fori_loop(1, ctx_count, cycle_turn, (state_now, own_block))
    running_max, running_sum, weighted = state_now
    heads_done = (weighted / running_sum[:, :, None]).astype(jnp.bfloat16)
    heads_done = jnp.transpose(heads_done, (1, 0, 2)).reshape(tok_query, device_share * HEAD_WIDTH)
    tok_rows, top_count = expert_ids.shape
    projected = lax.psum_scatter(
        jnp.dot(heads_done, out_weight, preferred_element_type=jnp.float32).astype(jnp.bfloat16),
        "exp",
        scatter_dimension=0,
        tiled=True,
    ).astype(jnp.float32)
    mixed = (residual.astype(jnp.float32) + projected).astype(jnp.bfloat16)
    stream = mixed.astype(jnp.float32)
    mean_sq = jnp.mean(stream * stream, axis=1, keepdims=True)
    normed = (stream * lax.rsqrt(mean_sq + eps_norm) * norm_gain[None, :]).astype(jnp.bfloat16)
    expert_count = lax.axis_size("exp")
    ctx_count = lax.axis_size("ctx")
    capacity = min(tok_rows, 2 * tok_rows * top_count // expert_count)
    slot_ids = slot_numbers(expert_ids)
    hits = route_hits(expert_ids, slot_ids, expert_count, capacity)
    send_table = jnp.any(hits, axis=3).astype(jnp.bfloat16)
    gate_local = w_gate[0]
    up_local = w_up[0]
    down_local = w_down[0]
    width = normed.shape[1]
    outgoing = jnp.einsum(
        "ecm,md->ecd", send_table, normed, preferred_element_type=jnp.float32
    ).astype(jnp.bfloat16)
    arrived = lax.all_to_all(outgoing, "exp", split_axis=0, concat_axis=0, tiled=True)
    local_rows = arrived.reshape(-1, width)
    hidden = expert_hidden(
        lax.all_gather(local_rows, "ctx", axis=0, tiled=True), gate_local, up_local
    )
    expert_result = jnp.dot(
        lax.all_gather(hidden, "ctx", axis=1, tiled=True),
        down_local,
        preferred_element_type=jnp.float32,
    ).astype(jnp.bfloat16)
    expert_result = expert_result.reshape(ctx_count, expert_count, capacity, down_local.shape[1])
    returned = lax.all_to_all(
        lax.all_to_all(expert_result, "ctx", split_axis=0, concat_axis=3, tiled=True),
        "exp",
        split_axis=1,
        concat_axis=0,
        tiled=True,
    )
    returned = returned.reshape(expert_count, capacity, width)
    mix_table = jnp.sum(jnp.where(hits, expert_gates[None, None, :, :], 0.0), axis=3)
    experts_out = jnp.einsum(
        "ecm,ecd->md", mix_table, returned.astype(jnp.float32), precision=lax.Precision.HIGHEST
    )
    return (mixed, experts_out.astype(jnp.bfloat16))


BF = jnp.bfloat16
F32 = jnp.float32
ROWS = 16
EXTRA = 128
PROJ_PARTS = 4
FF_PARTS = 3
OUT_PARTS = 2


def layer_kernel(
    queries,
    keys,
    values,
    residual,
    norm_gain,
    expert_ids,
    expert_gates,
    wo_hbm,
    wg_hbm,
    wu_hbm,
    wd_hbm,
    results,
    wo,
    wg,
    wu,
    wd,
    kv,
    res,
    table,
    heads,
    pc_send,
    pc_recv,
    px_send,
    px_recv,
    pz_send,
    pz_recv,
    proj,
    mixed_rows,
    rows_all,
    hidden,
    oc_send,
    oc_recv,
    ox_send,
    ox_recv,
    oz_send,
    oz_recv,
    eo,
    eo_recv,
    own_down,
    w_sem,
    send_sem,
    recv_sem,
):
    y = lax.axis_index("ctx")
    e = lax.axis_index("exp")
    z, x, k = e // 4, (e // 2) % 2, e % 2
    width = residual.shape[1]
    half = width // 2
    cols = half // PROJ_PARTS
    ff = hidden.shape[3]
    ff_cols = ff // FF_PARTS
    out_half = width // 4
    out_cols = out_half // OUT_PARTS
    tokens = queries.shape[0]

    def device(yy, zz, xx, kk):
        return (yy, zz * 4 + xx * 2 + kk)

    zs = (z, z + 1 - 2 * (z % 2), (z + 2) % 4, 3 - z)
    other_core = device(y, z, x, 1 - k)
    x_next = device(y, z, 1 - x, k)
    y_next = device(1 - y, z, x, k)
    partners = [other_core, x_next]
    for dy in range(2):
        for dz in range(4):
            if dy or dz:
                partners.append(device((y + dy) % 2, (z + dz) % 4, x, k))

    weight_copies = {}

    def fetch(name, src, dst):
        copy = pltpu.make_async_copy(src, dst, w_sem.at[len(weight_copies)])
        weight_copies[name] = copy
        copy.start()

    fetch("wo", wo_hbm, wo)

    barrier = pltpu.get_barrier_semaphore()
    for partner in partners:
        pl.semaphore_signal(barrier, inc=1, device_id=partner, device_id_type=pl.DeviceIdType.MESH)

    kvh = e * (queries.shape[1] // HEAD_WIDTH) // (QUERY_HEAD_COUNT // KEY_VALUE_HEADS)
    kv_cols = pl.ds(pl.multiple_of(kvh * HEAD_WIDTH, HEAD_WIDTH), HEAD_WIDTH)
    kv[y, 0] = keys[:, kv_cols]
    kv[y, 1] = values[:, kv_cols]
    res[k] = residual[...].astype(F32)
    lanes = lax.broadcasted_iota(jnp.int32, (expert_ids.shape[0], EXTRA), 1) % 64
    gate_rows = jnp.zeros(lanes.shape, F32)
    for slot in range(expert_ids.shape[1]):
        gate_rows += jnp.where(
            expert_ids[:, slot : slot + 1] == lanes, expert_gates[:, slot : slot + 1], 0.0
        )
    table[k] = gate_rows

    pl.semaphore_wait(barrier, len(partners))

    sent = []

    def send(src, dst, to):
        number = len(sent)
        copy = pltpu.make_async_remote_copy(
            src_ref=src,
            dst_ref=dst,
            send_sem=send_sem.at[number],
            recv_sem=recv_sem.at[number],
            device_id=to,
            device_id_type=pl.DeviceIdType.MESH,
        )
        copy.start()
        sent.append(copy)
        return copy

    kv_copy = send(kv.at[y], kv.at[y], y_next)
    res_copy = send(res.at[k], res.at[k], other_core)
    table_copy = send(table.at[k], table.at[k], other_core)

    kv_copy.wait_recv()
    key_all = kv[:, 0].reshape(2 * tokens, HEAD_WIDTH)
    value_all = kv[:, 1].reshape(2 * tokens, HEAD_WIDTH)
    shape = (tokens, 2 * tokens)
    allowed = lax.broadcasted_iota(jnp.int32, shape, 1) <= y * tokens + lax.broadcasted_iota(
        jnp.int32, shape, 0
    )
    scale = 1.0 / HEAD_WIDTH**0.5
    for head in range(queries.shape[1] // HEAD_WIDTH):
        span = slice(head * HEAD_WIDTH, (head + 1) * HEAD_WIDTH)
        scores = (
            lax.dot_general(
                queries[:, span], key_all, (((1,), (1,)), ((), ())), preferred_element_type=F32
            )
            * scale
        )
        scores = jnp.where(allowed, scores, neg_large)
        weights = jnp.where(
            allowed, jnp.exp(scores - jnp.max(scores, axis=1, keepdims=True)), 0.0
        )
        total = jnp.sum(weights, axis=1, keepdims=True)
        numer = jnp.dot(weights.astype(BF), value_all, preferred_element_type=F32)
        heads[:, span] = (numer / total).astype(BF)

    def columns(which, part, span, size):
        return pl.ds(pl.multiple_of(which * span + part * size, size), size)

    weight_copies["wo"].wait()
    to_core = []
    for part in range(PROJ_PARTS):
        piece = jnp.dot(
            heads[...], wo[:, columns(1 - k, part, half, cols)], preferred_element_type=F32
        )
        pc_send[part] = piece.astype(BF)
        to_core.append(send(pc_send.at[part], pc_recv.at[part], other_core))
    fetch("wg", wg_hbm.at[0], wg)
    to_x = []
    for part in range(PROJ_PARTS):
        piece = jnp.dot(
            heads[...], wo[:, columns(k, part, half, cols)], preferred_element_type=F32
        )
        to_core[part].wait_recv()
        piece = (piece + pc_recv[part].astype(F32)).astype(BF)
        for chip in range(tokens // ROWS):
            px_send[part, chip % 2, chip // 2] = piece[chip * ROWS : (chip + 1) * ROWS]
        to_x.append(send(px_send.at[part, 1 - x], px_recv.at[part], x_next))
    fetch("wu", wu_hbm.at[0], wu)
    to_z = []
    for part in range(PROJ_PARTS):
        to_x[part].wait_recv()
        pz_send[part] = (px_send[part, x].astype(F32) + px_recv[part].astype(F32)).astype(BF)
        for dz in range(1, 4):
            zz = (z + dz) % 4
            to_z.append(
                send(pz_send.at[part, zz], pz_recv.at[part, dz - 1], device(y, zz, x, k))
            )
    fetch("wd", wd_hbm.at[0], wd)
    back = []
    for part in range(PROJ_PARTS):
        piece = pz_send[part, z].astype(F32)
        for dz in range(1, 4):
            to_z[part * 3 + dz - 1].wait_recv()
            piece += pz_recv[part, dz - 1].astype(F32)
        place = columns(k, part, half, cols)
        proj[:, place] = piece
        back.append(send(proj.at[:, place], proj.at[:, place], other_core))

    res_copy.wait_recv()
    table_copy.wait_recv()
    for copy in back:
        copy.wait_recv()
    stream = (proj[...] + res[...].reshape(ROWS, width)).astype(BF).astype(F32)
    mean_sq = jnp.mean(stream * stream, axis=1, keepdims=True)
    normed = (stream * lax.rsqrt(mean_sq + eps_norm) * norm_gain[...]).astype(BF)
    gates = table[...].reshape(ROWS, EXTRA)
    gate_high = gates.astype(BF).astype(F32)
    gate_lane = lax.broadcasted_iota(jnp.int32, gates.shape, 1)
    gates = jnp.where(gate_lane < 64, gate_high, gates - gate_high).astype(BF)

    def block(xx, yy, zz):
        return ((zz // 2) * 4 + xx * 2 + yy) * 2 + zz % 2

    own = block(x, y, z)
    for side in range(2):
        rows_all[side, own, :, :half] = normed[:, side * half : (side + 1) * half]
        rows_all[side, own, :, half:] = gates

    def pass_on(number, to):
        place = rows_all.at[k, number]
        return send(place, place, to)

    y1, x1 = y + k * (1 - 2 * y), x + (1 - k) * (1 - 2 * x)
    y2, x2 = y + (1 - k) * (1 - 2 * y), x + k * (1 - 2 * x)
    first_to, second_to = device(y1, z, x1, k), device(y2, z, x2, k)
    along_z = [pass_on(own, device(y, zs[1], x, k))]
    first, second, second_far = {}, {}, {}
    cross = [[], []]
    first[0] = pass_on(own, first_to)
    second[0] = pass_on(own, second_to)
    along_z += [pass_on(own, device(y, zz, x, k)) for zz in zs[2:]]
    mixed_rows[...] = stream.reshape(2, ROWS // 2, width)
    results[0] = mixed_rows[k].astype(BF)

    def take_z(i):
        along_z[i - 1].wait_recv()
        number = block(x, y, zs[i])
        first[i] = pass_on(number, first_to)
        second[i] = pass_on(number, second_to)
        cross[i // 2].append(pass_on(number, other_core))

    def take_first(i):
        first[i].wait_recv()
        number = block(x1, y1, zs[i])
        second_far[i] = pass_on(number, second_to)
        cross[i // 2].append(pass_on(number, other_core))

    def take_second(i):
        second[i].wait_recv()
        cross[i // 2].append(pass_on(block(x2, y2, zs[i]), other_core))

    def take_far(i):
        second_far[i].wait_recv()
        cross[i // 2].append(pass_on(block(1 - x, 1 - y, zs[i]), other_core))

    chunk_tokens = tokens
    chunk_blocks = chunk_tokens // ROWS
    across = [[], []]

    def chunk_rows(chunk):
        pair = z // 2 + chunk * (1 - 2 * (z // 2))
        return pl.ds(pair * chunk_blocks, chunk_blocks)

    def expert_up(chunk, part):
        span = slice(part * ff_cols, (part + 1) * ff_cols)
        gate = jnp.zeros((chunk_tokens, ff_cols), F32)
        upper = jnp.zeros((chunk_tokens, ff_cols), F32)
        for side in range(2):
            rows = rows_all[side, chunk_rows(chunk), :, :half].reshape(chunk_tokens, half)
            depth = slice(side * half, (side + 1) * half)
            gate += jnp.dot(rows, wg[depth, span], preferred_element_type=F32)
            upper += jnp.dot(rows, wu[depth, span], preferred_element_type=F32)
        hidden[chunk, y, :, span] = (gate / (1.0 + jnp.exp(-gate)) * upper).astype(BF)
        place = hidden.at[chunk, y, :, span]
        across[chunk].append(send(place, place, y_next))

    take_z(1)
    take_first(0)
    take_second(0)
    take_z(2)
    take_first(1)
    take_second(1)
    take_z(3)
    take_far(0)
    take_far(1)
    weight_copies["wg"].wait()
    weight_copies["wu"].wait()
    for copy in cross[0]:
        copy.wait_recv()
    expert_up(0, 0)
    take_first(2)
    take_second(2)
    for part in range(1, FF_PARTS):
        expert_up(0, part)
        if part == 1:
            take_first(3)
            take_second(3)
    take_far(2)
    take_far(3)
    for copy in cross[1]:
        copy.wait_recv()
    for part in range(FF_PARTS):
        expert_up(1, part)

    shares = []
    for chunk in range(2):
        picked = rows_all[0, chunk_rows(chunk), :, half:].reshape(chunk_tokens, EXTRA).astype(F32)
        picked_lane = lax.broadcasted_iota(jnp.int32, picked.shape, 1) % 64
        shares.append(jnp.sum(jnp.where(picked_lane == e, picked, 0.0), axis=1, keepdims=True))
    weight_copies["wd"].wait()

    own_depth = pl.ds(pl.multiple_of(y * ff, ff), ff)
    far_depth = pl.ds(pl.multiple_of((1 - y) * ff, ff), ff)

    def down_own(chunk):
        for which in range(2 * OUT_PARTS):
            span = slice(which * out_cols, (which + 1) * out_cols)
            own_down[which] = jnp.dot(
                hidden[chunk, y], wd[own_depth, span], preferred_element_type=F32
            )

    def down(chunk, which, part):
        place = columns(which, part, out_half, out_cols)
        result = jnp.dot(hidden[chunk, 1 - y], wd[far_depth, place], preferred_element_type=F32)
        if chunk:
            result += own_down[which * OUT_PARTS + part]
        else:
            result += jnp.dot(hidden[chunk, y], wd[own_depth, place], preferred_element_type=F32)
        return result * shares[chunk]

    to_x, to_z = {}, {}

    def outputs_to_core(chunk):
        for copy in across[chunk]:
            copy.wait_recv()
        to_core = []
        for part in range(OUT_PARTS):
            oc_send[chunk, part] = down(chunk, 1 - k, part).astype(BF)
            to_core.append(send(oc_send.at[chunk, part], oc_recv.at[chunk, part], other_core))
        return to_core

    def outputs_to_x(chunk, to_core):
        for part in range(OUT_PARTS):
            piece = down(chunk, k, part)
            to_core[part].wait_recv()
            piece = (piece + oc_recv[chunk, part].astype(F32)).astype(BF)
            ox_send[chunk, part] = piece.reshape(2, 2, 2, ROWS, out_cols)
            to_x[chunk, part] = send(
                ox_send.at[chunk, part, 1 - x], ox_recv.at[chunk, part], x_next
            )

    def outputs_to_z(chunk):
        for part in range(OUT_PARTS):
            to_x[chunk, part].wait_recv()
            oz_send[chunk, part] = (
                ox_send[chunk, part, x].astype(F32) + ox_recv[chunk, part].astype(F32)
            ).astype(BF)
            for dy in range(2):
                for dz in (2 * chunk, 2 * chunk + 1):
                    if dy or dz:
                        yy = y + dy * (1 - 2 * y)
                        to_z[part, dy, dz] = send(
                            oz_send.at[chunk, part, yy, zs[dz] % 2],
                            oz_recv.at[part, dy * 4 + dz],
                            device(yy, zs[dz], x, k),
                        )

    outputs_to_x(0, outputs_to_core(0))
    down_own(1)
    to_core = outputs_to_core(1)
    outputs_to_z(0)
    outputs_to_x(1, to_core)
    outputs_to_z(1)
    back = []
    for part in range(OUT_PARTS):
        for dy in range(2):
            piece = None
            for dz in range(4):
                if (part, dy, dz) not in to_z:
                    piece = oz_send[0, part, y, z % 2].astype(F32)
                    continue
                to_z[part, dy, dz].wait_recv()
                came = oz_recv[part, dy * 4 + dz].astype(F32)
                piece = came if piece is None else piece + came
            side = y + dy * (1 - 2 * y)
            place = columns(side * 2 + k, part, out_half, out_cols)
            eo[:, :, place] = piece.reshape(2, ROWS // 2, out_cols)
            back.append(send(eo.at[1 - k, :, place], eo_recv.at[:, place], other_core))
    for part in range(OUT_PARTS):
        for side in range(2):
            place = columns(side * 2 + k, part, out_half, out_cols)
            results[1, :, place] = eo[k, :, place].astype(BF)
    for copy in back:
        copy.wait_recv()
    for part in range(OUT_PARTS):
        for side in range(2):
            place = columns(side * 2 + 1 - k, part, out_half, out_cols)
            results[1, :, place] = eo_recv[:, place].astype(BF)
    for copy in sent:
        copy.wait_send()


def layer_on_device(
    queries,
    keys,
    values,
    residual,
    out_weight,
    norm_gain,
    expert_ids,
    expert_gates,
    w_gate,
    w_up,
    w_down,
):
    tokens, head_cols = queries.shape
    own_rows, width = residual.shape
    ff = w_gate.shape[2]
    half = width // 2
    cols = half // PROJ_PARTS
    out_cols = width // 4 // OUT_PARTS
    all_tokens = 2 * tokens
    vmem = pl.BlockSpec(memory_space=pltpu.VMEM)
    hbm = pl.BlockSpec(memory_space=pl.ANY)
    scratch = [
        pltpu.VMEM(out_weight.shape, BF),
        pltpu.VMEM(w_gate.shape[1:], BF),
        pltpu.VMEM(w_up.shape[1:], BF),
        pltpu.VMEM(w_down.shape[1:], BF),
        pltpu.VMEM((2, 2, tokens, HEAD_WIDTH), BF),
        pltpu.VMEM((2, own_rows, width), F32),
        pltpu.VMEM((2, own_rows, EXTRA), F32),
        pltpu.VMEM((tokens, head_cols), BF),
        pltpu.VMEM((PROJ_PARTS, tokens, cols), BF),
        pltpu.VMEM((PROJ_PARTS, tokens, cols), BF),
        pltpu.VMEM((PROJ_PARTS, 2, 4, ROWS, cols), BF),
        pltpu.VMEM((PROJ_PARTS, 4, ROWS, cols), BF),
        pltpu.VMEM((PROJ_PARTS, 4, ROWS, cols), BF),
        pltpu.VMEM((PROJ_PARTS, 3, ROWS, cols), BF),
        pltpu.VMEM((ROWS, width), F32),
        pltpu.VMEM((2, own_rows, width), F32),
        pltpu.VMEM((2, 16, ROWS, half + EXTRA), BF),
        pltpu.VMEM((2, 2, tokens, ff), BF),
        pltpu.VMEM((2, OUT_PARTS, tokens, out_cols), BF),
        pltpu.VMEM((2, OUT_PARTS, tokens, out_cols), BF),
        pltpu.VMEM((2, OUT_PARTS, 2, 2, 2, ROWS, out_cols), BF),
        pltpu.VMEM((2, OUT_PARTS, 2, 2, ROWS, out_cols), BF),
        pltpu.VMEM((2, OUT_PARTS, 2, 2, ROWS, out_cols), BF),
        pltpu.VMEM((OUT_PARTS, 8, ROWS, out_cols), BF),
        pltpu.VMEM((2, own_rows, width), F32),
        pltpu.VMEM((own_rows, width), F32),
        pltpu.VMEM((2 * OUT_PARTS, tokens, out_cols), F32),
        pltpu.SemaphoreType.DMA((16,)),
        pltpu.SemaphoreType.DMA((96,)),
        pltpu.SemaphoreType.DMA((96,)),
    ]
    flops = 2 * all_tokens * width * ff * 4 + 2 * tokens * head_cols * width
    results = pl.pallas_call(
        layer_kernel,
        out_shape=jax.ShapeDtypeStruct((2, own_rows, width), BF),
        in_specs=[vmem] * 7 + [hbm] * 4,
        out_specs=vmem,
        scratch_shapes=scratch,
        compiler_params=pltpu.CompilerParams(
            collective_id=0, has_side_effects=True, vmem_limit_bytes=56 * 2**20
        ),
        cost_estimate=pl.CostEstimate(
            flops=flops, bytes_accessed=24 * 2**20, transcendentals=2**18
        ),
    )(
        queries,
        keys,
        values,
        residual,
        norm_gain.reshape(1, width),
        expert_ids,
        expert_gates,
        out_weight,
        w_gate,
        w_up,
        w_down,
    )
    return results[0], results[1]


def solution(mesh):
    one_block = mesh.shape["ctx"] == 2 and mesh.shape["exp"] == 16
    return jax.shard_map(
        layer_on_device if one_block else on_device,
        mesh=mesh,
        in_specs=(
            P("ctx", "exp"),
            P("ctx", None),
            P("ctx", None),
            P(("ctx", "exp"), None),
            P("exp", None),
            P(),
            P(("ctx", "exp"), None),
            P(("ctx", "exp"), None),
            P("exp", None, "ctx"),
            P("exp", None, "ctx"),
            P("exp", None, "ctx"),
        ),
        out_specs=(P(("ctx", "exp"), None), P(("ctx", "exp"), None)),
        check_vma=False,
    )
```

```python
import jax
import jax.numpy as jnp
from jax import lax
from jax.experimental import pallas as pl
from jax.experimental.pallas import tpu as pltpu
from jax.sharding import PartitionSpec as P

QUERY_HEAD_COUNT = 64
KEY_VALUE_HEADS = 4
HEAD_WIDTH = 128


neg_large = -1e30
eps_norm = 1e-06


def shifted(value, axis, by):
    size = lax.axis_size(axis)
    pairs = [(i, i + by) for i in range(size) if 0 <= i + by < size]
    return lax.ppermute(value, axis, pairs)


def slot_numbers(expert_ids):
    tok_rows, top_count = expert_ids.shape
    flat_ids = expert_ids.reshape(-1)
    owner_row = jnp.arange(tok_rows * top_count, dtype=jnp.int32) // top_count
    earlier = (flat_ids[:, None] == flat_ids[None, :]) & (owner_row[None, :] < owner_row[:, None])
    return jnp.sum(earlier.astype(jnp.int32), axis=1).reshape(tok_rows, top_count)


def route_hits(expert_ids, slot_ids, expert_count, capacity):
    expert_hit = (
        expert_ids[None, None, :, :]
        == jnp.arange(expert_count, dtype=jnp.int32)[:, None, None, None]
    )
    slot_hit = (
        slot_ids[None, None, :, :] == jnp.arange(capacity, dtype=jnp.int32)[None, :, None, None]
    )
    return expert_hit & slot_hit


def expert_hidden(rows_block, gate_local, up_local):
    gate = jnp.dot(rows_block, gate_local, preferred_element_type=jnp.float32)
    upper = jnp.dot(rows_block, up_local, preferred_element_type=jnp.float32)
    return (jax.nn.silu(gate) * upper).astype(jnp.bfloat16)


def on_device(
    queries,
    keys,
    values,
    residual,
    out_weight,
    norm_gain,
    expert_ids,
    expert_gates,
    w_gate,
    w_up,
    w_down,
):
    tok_query = queries.shape[0]
    device_share = queries.shape[1] // HEAD_WIDTH
    ctx_pos = lax.axis_index("ctx")
    key_value_head = lax.axis_index("exp") * device_share // (QUERY_HEAD_COUNT // KEY_VALUE_HEADS)
    own_keys = lax.dynamic_slice_in_dim(keys, key_value_head * HEAD_WIDTH, HEAD_WIDTH, 1)
    own_values = lax.dynamic_slice_in_dim(values, key_value_head * HEAD_WIDTH, HEAD_WIDTH, 1)
    own_block = jnp.stack([own_keys, own_values])
    query_heads = queries.reshape(tok_query, device_share, HEAD_WIDTH)
    query_start = ctx_pos * tok_query
    query_pos = query_start + jnp.arange(tok_query, dtype=jnp.int32)
    scale = 1.0 / HEAD_WIDTH**0.5
    start_state = (
        jnp.full((device_share, tok_query), neg_large, jnp.float32),
        jnp.zeros((device_share, tok_query), jnp.float32),
        jnp.zeros((device_share, tok_query, HEAD_WIDTH), jnp.float32),
    )

    def attend(state_now, kv_piece, key_start):

        def compute(current):
            running_max, running_sum, weighted = current
            key_pos = key_start + jnp.arange(kv_piece.shape[1], dtype=jnp.int32)
            allowed = key_pos[None, :] <= query_pos[:, None]
            scores = (
                jnp.einsum(
                    "qhd,kd->hqk", query_heads, kv_piece[0], preferred_element_type=jnp.float32
                )
                * scale
            )
            scores = jnp.where(allowed[None], scores, neg_large)
            new_max = jnp.maximum(running_max, jnp.max(scores, axis=2))
            weights_blk = jnp.where(allowed[None], jnp.exp(scores - new_max[:, :, None]), 0.0)
            shrink = jnp.exp(running_max - new_max)
            new_sum = running_sum * shrink + jnp.sum(weights_blk, axis=2)
            added = jnp.einsum(
                "hqk,kd->hqd",
                weights_blk.astype(jnp.bfloat16),
                kv_piece[1],
                preferred_element_type=jnp.float32,
            )
            return (new_max, new_sum, weighted * shrink[:, :, None] + added)

        def unchanged(current):
            return current

        useful = (key_start >= 0) & (key_start <= query_start + tok_query - 1)
        return lax.cond(useful, compute, unchanged, state_now)

    ctx_count = lax.axis_size("ctx")
    state_now = attend(start_state, own_block, query_start)

    def cycle_turn(cycle_step, carried):
        state_cur, moving = carried
        moving = shifted(moving, "ctx", 1)
        source = ctx_pos - cycle_step
        return (attend(state_cur, moving, source * tok_query), moving)

    state_now, _ = lax.fori_loop(1, ctx_count, cycle_turn, (state_now, own_block))
    running_max, running_sum, weighted = state_now
    heads_done = (weighted / running_sum[:, :, None]).astype(jnp.bfloat16)
    heads_done = jnp.transpose(heads_done, (1, 0, 2)).reshape(tok_query, device_share * HEAD_WIDTH)
    tok_rows, top_count = expert_ids.shape
    projected = lax.psum_scatter(
        jnp.dot(heads_done, out_weight, preferred_element_type=jnp.float32).astype(jnp.bfloat16),
        "exp",
        scatter_dimension=0,
        tiled=True,
    ).astype(jnp.float32)
    mixed = (residual.astype(jnp.float32) + projected).astype(jnp.bfloat16)
    stream = mixed.astype(jnp.float32)
    mean_sq = jnp.mean(stream * stream, axis=1, keepdims=True)
    normed = (stream * lax.rsqrt(mean_sq + eps_norm) * norm_gain[None, :]).astype(jnp.bfloat16)
    expert_count = lax.axis_size("exp")
    ctx_count = lax.axis_size("ctx")
    capacity = min(tok_rows, 2 * tok_rows * top_count // expert_count)
    slot_ids = slot_numbers(expert_ids)
    hits = route_hits(expert_ids, slot_ids, expert_count, capacity)
    send_table = jnp.any(hits, axis=3).astype(jnp.bfloat16)
    gate_local = w_gate[0]
    up_local = w_up[0]
    down_local = w_down[0]
    width = normed.shape[1]
    outgoing = jnp.einsum(
        "ecm,md->ecd", send_table, normed, preferred_element_type=jnp.float32
    ).astype(jnp.bfloat16)
    arrived = lax.all_to_all(outgoing, "exp", split_axis=0, concat_axis=0, tiled=True)
    local_rows = arrived.reshape(-1, width)
    hidden = expert_hidden(
        lax.all_gather(local_rows, "ctx", axis=0, tiled=True), gate_local, up_local
    )
    expert_result = jnp.dot(
        lax.all_gather(hidden, "ctx", axis=1, tiled=True),
        down_local,
        preferred_element_type=jnp.float32,
    ).astype(jnp.bfloat16)
    expert_result = expert_result.reshape(ctx_count, expert_count, capacity, down_local.shape[1])
    returned = lax.all_to_all(
        lax.all_to_all(expert_result, "ctx", split_axis=0, concat_axis=3, tiled=True),
        "exp",
        split_axis=1,
        concat_axis=0,
        tiled=True,
    )
    returned = returned.reshape(expert_count, capacity, width)
    mix_table = jnp.sum(jnp.where(hits, expert_gates[None, None, :, :], 0.0), axis=3)
    experts_out = jnp.einsum(
        "ecm,ecd->md", mix_table, returned.astype(jnp.float32), precision=lax.Precision.HIGHEST
    )
    return (mixed, experts_out.astype(jnp.bfloat16))


BF = jnp.bfloat16
F32 = jnp.float32
ROWS = 16
EXTRA = 128
PROJ_PARTS = 8
FF_PARTS = 3
OUT_PARTS = 2


def layer_kernel(
    queries,
    keys,
    values,
    residual,
    norm_gain,
    expert_ids,
    expert_gates,
    wo_hbm,
    wg_hbm,
    wu_hbm,
    wd_hbm,
    results,
    wo,
    wg,
    wu,
    wd,
    kv,
    res,
    table,
    heads,
    pc_send,
    pc_recv,
    px_send,
    px_recv,
    pz_send,
    pz_recv,
    proj,
    mixed_rows,
    rows_all,
    hidden,
    oc_send,
    oc_recv,
    ox_send,
    ox_recv,
    oz_send,
    oz_recv,
    eo,
    eo_recv,
    own_down,
    w_sem,
    send_sem,
    recv_sem,
):
    y = lax.axis_index("ctx")
    e = lax.axis_index("exp")
    z, x, k = e // 4, (e // 2) % 2, e % 2
    width = residual.shape[1]
    half = width // 2
    cols = half // PROJ_PARTS
    ff = hidden.shape[3]
    ff_cols = ff // FF_PARTS
    out_half = width // 4
    out_cols = out_half // OUT_PARTS
    tokens = queries.shape[0]

    def device(yy, zz, xx, kk):
        return (yy, zz * 4 + xx * 2 + kk)

    zs = (z, z + 1 - 2 * (z % 2), (z + 2) % 4, 3 - z)
    other_core = device(y, z, x, 1 - k)
    x_next = device(y, z, 1 - x, k)
    y_next = device(1 - y, z, x, k)
    partners = [other_core, x_next]
    for dy in range(2):
        for dz in range(4):
            if dy or dz:
                partners.append(device((y + dy) % 2, (z + dz) % 4, x, k))

    weight_copies = {}

    def fetch(name, src, dst):
        copy = pltpu.make_async_copy(src, dst, w_sem.at[len(weight_copies)])
        weight_copies[name] = copy
        copy.start()

    fetch("wo", wo_hbm, wo)

    barrier = pltpu.get_barrier_semaphore()
    for partner in partners:
        pl.semaphore_signal(barrier, inc=1, device_id=partner, device_id_type=pl.DeviceIdType.MESH)

    kvh = e * (queries.shape[1] // HEAD_WIDTH) // (QUERY_HEAD_COUNT // KEY_VALUE_HEADS)
    kv_cols = pl.ds(pl.multiple_of(kvh * HEAD_WIDTH, HEAD_WIDTH), HEAD_WIDTH)
    kv[y, 0] = keys[:, kv_cols]
    kv[y, 1] = values[:, kv_cols]
    res[k] = residual[...].astype(F32)
    lanes = lax.broadcasted_iota(jnp.int32, (expert_ids.shape[0], EXTRA), 1) % 64
    gate_rows = jnp.zeros(lanes.shape, F32)
    for slot in range(expert_ids.shape[1]):
        gate_rows += jnp.where(
            expert_ids[:, slot : slot + 1] == lanes, expert_gates[:, slot : slot + 1], 0.0
        )
    table[k] = gate_rows

    pl.semaphore_wait(barrier, len(partners))

    sent = []

    def send(src, dst, to):
        number = len(sent)
        copy = pltpu.make_async_remote_copy(
            src_ref=src,
            dst_ref=dst,
            send_sem=send_sem.at[number],
            recv_sem=recv_sem.at[number],
            device_id=to,
            device_id_type=pl.DeviceIdType.MESH,
        )
        copy.start()
        sent.append(copy)
        return copy

    kv_copy = send(kv.at[y], kv.at[y], y_next)
    res_copy = send(res.at[k], res.at[k], other_core)
    table_copy = send(table.at[k], table.at[k], other_core)

    kv_copy.wait_recv()
    key_all = kv[:, 0].reshape(2 * tokens, HEAD_WIDTH)
    value_all = kv[:, 1].reshape(2 * tokens, HEAD_WIDTH)
    shape = (tokens, 2 * tokens)
    allowed = lax.broadcasted_iota(jnp.int32, shape, 1) <= y * tokens + lax.broadcasted_iota(
        jnp.int32, shape, 0
    )
    scale = 1.0 / HEAD_WIDTH**0.5
    for head in range(queries.shape[1] // HEAD_WIDTH):
        span = slice(head * HEAD_WIDTH, (head + 1) * HEAD_WIDTH)
        scores = (
            lax.dot_general(
                queries[:, span], key_all, (((1,), (1,)), ((), ())), preferred_element_type=F32
            )
            * scale
        )
        scores = jnp.where(allowed, scores, neg_large)
        weights = jnp.where(
            allowed, jnp.exp(scores - jnp.max(scores, axis=1, keepdims=True)), 0.0
        )
        total = jnp.sum(weights, axis=1, keepdims=True)
        numer = jnp.dot(weights.astype(BF), value_all, preferred_element_type=F32)
        heads[:, span] = (numer / total).astype(BF)

    def columns(which, part, span, size):
        return pl.ds(pl.multiple_of(which * span + part * size, size), size)

    weight_copies["wo"].wait()
    to_core = []
    for part in range(PROJ_PARTS):
        piece = jnp.dot(
            heads[...], wo[:, columns(1 - k, part, half, cols)], preferred_element_type=F32
        )
        pc_send[part] = piece.astype(BF)
        to_core.append(send(pc_send.at[part], pc_recv.at[part], other_core))
    fetch("wg", wg_hbm.at[0], wg)
    to_x = []
    for part in range(PROJ_PARTS):
        piece = jnp.dot(
            heads[...], wo[:, columns(k, part, half, cols)], preferred_element_type=F32
        )
        to_core[part].wait_recv()
        piece = (piece + pc_recv[part].astype(F32)).astype(BF)
        for chip in range(tokens // ROWS):
            px_send[part, chip % 2, chip // 2] = piece[chip * ROWS : (chip + 1) * ROWS]
        to_x.append(send(px_send.at[part, 1 - x], px_recv.at[part], x_next))
    fetch("wu", wu_hbm.at[0], wu)
    to_z = []
    for part in range(PROJ_PARTS):
        to_x[part].wait_recv()
        pz_send[part] = (px_send[part, x].astype(F32) + px_recv[part].astype(F32)).astype(BF)
        for dz in range(1, 4):
            zz = (z + dz) % 4
            to_z.append(
                send(pz_send.at[part, zz], pz_recv.at[part, dz - 1], device(y, zz, x, k))
            )
    fetch("wd", wd_hbm.at[0], wd)
    back = []
    for part in range(PROJ_PARTS):
        piece = pz_send[part, z].astype(F32)
        for dz in range(1, 4):
            to_z[part * 3 + dz - 1].wait_recv()
            piece += pz_recv[part, dz - 1].astype(F32)
        place = columns(k, part, half, cols)
        proj[:, place] = piece
        back.append(send(proj.at[:, place], proj.at[:, place], other_core))

    res_copy.wait_recv()
    table_copy.wait_recv()
    for copy in back:
        copy.wait_recv()
    stream = (proj[...] + res[...].reshape(ROWS, width)).astype(BF).astype(F32)
    mean_sq = jnp.mean(stream * stream, axis=1, keepdims=True)
    normed = (stream * lax.rsqrt(mean_sq + eps_norm) * norm_gain[...]).astype(BF)
    gates = table[...].reshape(ROWS, EXTRA)
    gate_high = gates.astype(BF).astype(F32)
    gate_lane = lax.broadcasted_iota(jnp.int32, gates.shape, 1)
    gates = jnp.where(gate_lane < 64, gate_high, gates - gate_high).astype(BF)

    def block(xx, yy, zz):
        return ((zz // 2) * 4 + xx * 2 + yy) * 2 + zz % 2

    own = block(x, y, z)
    for side in range(2):
        rows_all[side, own, :, :half] = normed[:, side * half : (side + 1) * half]
        rows_all[side, own, :, half:] = gates

    def pass_on(number, to):
        place = rows_all.at[k, number]
        return send(place, place, to)

    y1, x1 = y + k * (1 - 2 * y), x + (1 - k) * (1 - 2 * x)
    y2, x2 = y + (1 - k) * (1 - 2 * y), x + k * (1 - 2 * x)
    first_to, second_to = device(y1, z, x1, k), device(y2, z, x2, k)
    along_z = [pass_on(own, device(y, zs[1], x, k))]
    first, second, second_far = {}, {}, {}
    cross = [[], []]
    first[0] = pass_on(own, first_to)
    second[0] = pass_on(own, second_to)
    along_z += [pass_on(own, device(y, zz, x, k)) for zz in zs[2:]]
    mixed_rows[...] = stream.reshape(2, ROWS // 2, width)
    results[0] = mixed_rows[k].astype(BF)

    def take_z(i):
        along_z[i - 1].wait_recv()
        number = block(x, y, zs[i])
        first[i] = pass_on(number, first_to)
        second[i] = pass_on(number, second_to)
        cross[i // 2].append(pass_on(number, other_core))

    def take_first(i):
        first[i].wait_recv()
        number = block(x1, y1, zs[i])
        second_far[i] = pass_on(number, second_to)
        cross[i // 2].append(pass_on(number, other_core))

    def take_second(i):
        second[i].wait_recv()
        cross[i // 2].append(pass_on(block(x2, y2, zs[i]), other_core))

    def take_far(i):
        second_far[i].wait_recv()
        cross[i // 2].append(pass_on(block(1 - x, 1 - y, zs[i]), other_core))

    chunk_tokens = tokens
    chunk_blocks = chunk_tokens // ROWS
    across = [[], []]

    def chunk_rows(chunk):
        pair = z // 2 + chunk * (1 - 2 * (z // 2))
        return pl.ds(pair * chunk_blocks, chunk_blocks)

    def expert_up(chunk, part):
        span = slice(part * ff_cols, (part + 1) * ff_cols)
        gate = jnp.zeros((chunk_tokens, ff_cols), F32)
        upper = jnp.zeros((chunk_tokens, ff_cols), F32)
        for side in range(2):
            rows = rows_all[side, chunk_rows(chunk), :, :half].reshape(chunk_tokens, half)
            depth = slice(side * half, (side + 1) * half)
            gate += jnp.dot(rows, wg[depth, span], preferred_element_type=F32)
            upper += jnp.dot(rows, wu[depth, span], preferred_element_type=F32)
        hidden[chunk, y, :, span] = (gate / (1.0 + jnp.exp(-gate)) * upper).astype(BF)
        place = hidden.at[chunk, y, :, span]
        across[chunk].append(send(place, place, y_next))

    take_z(1)
    take_first(0)
    take_second(0)
    take_z(2)
    take_first(1)
    take_second(1)
    take_z(3)
    take_far(0)
    take_far(1)
    weight_copies["wg"].wait()
    weight_copies["wu"].wait()
    for copy in cross[0]:
        copy.wait_recv()
    expert_up(0, 0)
    take_first(2)
    take_second(2)
    for part in range(1, FF_PARTS):
        expert_up(0, part)
        if part == 1:
            take_first(3)
            take_second(3)
    take_far(2)
    take_far(3)
    for copy in cross[1]:
        copy.wait_recv()
    for part in range(FF_PARTS):
        expert_up(1, part)

    shares = []
    for chunk in range(2):
        picked = rows_all[0, chunk_rows(chunk), :, half:].reshape(chunk_tokens, EXTRA).astype(F32)
        picked_lane = lax.broadcasted_iota(jnp.int32, picked.shape, 1) % 64
        shares.append(jnp.sum(jnp.where(picked_lane == e, picked, 0.0), axis=1, keepdims=True))
    weight_copies["wd"].wait()

    own_depth = pl.ds(pl.multiple_of(y * ff, ff), ff)
    far_depth = pl.ds(pl.multiple_of((1 - y) * ff, ff), ff)

    def down_own(chunk):
        for which in range(2 * OUT_PARTS):
            span = slice(which * out_cols, (which + 1) * out_cols)
            own_down[which] = jnp.dot(
                hidden[chunk, y], wd[own_depth, span], preferred_element_type=F32
            )

    def down(chunk, which, part):
        place = columns(which, part, out_half, out_cols)
        result = jnp.dot(hidden[chunk, 1 - y], wd[far_depth, place], preferred_element_type=F32)
        if chunk:
            result += own_down[which * OUT_PARTS + part]
        else:
            result += jnp.dot(hidden[chunk, y], wd[own_depth, place], preferred_element_type=F32)
        return result * shares[chunk]

    to_x, to_z = {}, {}

    def outputs_to_core(chunk):
        for copy in across[chunk]:
            copy.wait_recv()
        to_core = []
        for part in range(OUT_PARTS):
            oc_send[chunk, part] = down(chunk, 1 - k, part).astype(BF)
            to_core.append(send(oc_send.at[chunk, part], oc_recv.at[chunk, part], other_core))
        return to_core

    def outputs_to_x(chunk, to_core):
        for part in range(OUT_PARTS):
            piece = down(chunk, k, part)
            to_core[part].wait_recv()
            piece = (piece + oc_recv[chunk, part].astype(F32)).astype(BF)
            ox_send[chunk, part] = piece.reshape(2, 2, 2, ROWS, out_cols)
            to_x[chunk, part] = send(
                ox_send.at[chunk, part, 1 - x], ox_recv.at[chunk, part], x_next
            )

    def outputs_to_z(chunk):
        for part in range(OUT_PARTS):
            to_x[chunk, part].wait_recv()
            oz_send[chunk, part] = (
                ox_send[chunk, part, x].astype(F32) + ox_recv[chunk, part].astype(F32)
            ).astype(BF)
            for dy in range(2):
                for dz in (2 * chunk, 2 * chunk + 1):
                    if dy or dz:
                        yy = y + dy * (1 - 2 * y)
                        to_z[part, dy, dz] = send(
                            oz_send.at[chunk, part, yy, zs[dz] % 2],
                            oz_recv.at[part, dy * 4 + dz],
                            device(yy, zs[dz], x, k),
                        )

    outputs_to_x(0, outputs_to_core(0))
    down_own(1)
    to_core = outputs_to_core(1)
    outputs_to_z(0)
    outputs_to_x(1, to_core)
    outputs_to_z(1)
    back = []
    for part in range(OUT_PARTS):
        for dy in range(2):
            piece = None
            for dz in range(4):
                if (part, dy, dz) not in to_z:
                    piece = oz_send[0, part, y, z % 2].astype(F32)
                    continue
                to_z[part, dy, dz].wait_recv()
                came = oz_recv[part, dy * 4 + dz].astype(F32)
                piece = came if piece is None else piece + came
            side = y + dy * (1 - 2 * y)
            place = columns(side * 2 + k, part, out_half, out_cols)
            eo[:, :, place] = piece.reshape(2, ROWS // 2, out_cols)
            back.append(send(eo.at[1 - k, :, place], eo_recv.at[:, place], other_core))
    for part in range(OUT_PARTS):
        for side in range(2):
            place = columns(side * 2 + k, part, out_half, out_cols)
            results[1, :, place] = eo[k, :, place].astype(BF)
    for copy in back:
        copy.wait_recv()
    for part in range(OUT_PARTS):
        for side in range(2):
            place = columns(side * 2 + 1 - k, part, out_half, out_cols)
            results[1, :, place] = eo_recv[:, place].astype(BF)
    for copy in sent:
        copy.wait_send()


def layer_on_device(
    queries,
    keys,
    values,
    residual,
    out_weight,
    norm_gain,
    expert_ids,
    expert_gates,
    w_gate,
    w_up,
    w_down,
):
    tokens, head_cols = queries.shape
    own_rows, width = residual.shape
    ff = w_gate.shape[2]
    half = width // 2
    cols = half // PROJ_PARTS
    out_cols = width // 4 // OUT_PARTS
    all_tokens = 2 * tokens
    vmem = pl.BlockSpec(memory_space=pltpu.VMEM)
    hbm = pl.BlockSpec(memory_space=pl.ANY)
    scratch = [
        pltpu.VMEM(out_weight.shape, BF),
        pltpu.VMEM(w_gate.shape[1:], BF),
        pltpu.VMEM(w_up.shape[1:], BF),
        pltpu.VMEM(w_down.shape[1:], BF),
        pltpu.VMEM((2, 2, tokens, HEAD_WIDTH), BF),
        pltpu.VMEM((2, own_rows, width), F32),
        pltpu.VMEM((2, own_rows, EXTRA), F32),
        pltpu.VMEM((tokens, head_cols), BF),
        pltpu.VMEM((PROJ_PARTS, tokens, cols), BF),
        pltpu.VMEM((PROJ_PARTS, tokens, cols), BF),
        pltpu.VMEM((PROJ_PARTS, 2, 4, ROWS, cols), BF),
        pltpu.VMEM((PROJ_PARTS, 4, ROWS, cols), BF),
        pltpu.VMEM((PROJ_PARTS, 4, ROWS, cols), BF),
        pltpu.VMEM((PROJ_PARTS, 3, ROWS, cols), BF),
        pltpu.VMEM((ROWS, width), F32),
        pltpu.VMEM((2, own_rows, width), F32),
        pltpu.VMEM((2, 16, ROWS, half + EXTRA), BF),
        pltpu.VMEM((2, 2, tokens, ff), BF),
        pltpu.VMEM((2, OUT_PARTS, tokens, out_cols), BF),
        pltpu.VMEM((2, OUT_PARTS, tokens, out_cols), BF),
        pltpu.VMEM((2, OUT_PARTS, 2, 2, 2, ROWS, out_cols), BF),
        pltpu.VMEM((2, OUT_PARTS, 2, 2, ROWS, out_cols), BF),
        pltpu.VMEM((2, OUT_PARTS, 2, 2, ROWS, out_cols), BF),
        pltpu.VMEM((OUT_PARTS, 8, ROWS, out_cols), BF),
        pltpu.VMEM((2, own_rows, width), F32),
        pltpu.VMEM((own_rows, width), F32),
        pltpu.VMEM((2 * OUT_PARTS, tokens, out_cols), F32),
        pltpu.SemaphoreType.DMA((16,)),
        pltpu.SemaphoreType.DMA((128,)),
        pltpu.SemaphoreType.DMA((128,)),
    ]
    flops = 2 * all_tokens * width * ff * 4 + 2 * tokens * head_cols * width
    results = pl.pallas_call(
        layer_kernel,
        out_shape=jax.ShapeDtypeStruct((2, own_rows, width), BF),
        in_specs=[vmem] * 7 + [hbm] * 4,
        out_specs=vmem,
        scratch_shapes=scratch,
        compiler_params=pltpu.CompilerParams(
            collective_id=0, has_side_effects=True, vmem_limit_bytes=56 * 2**20
        ),
        cost_estimate=pl.CostEstimate(
            flops=flops, bytes_accessed=24 * 2**20, transcendentals=2**18
        ),
    )(
        queries,
        keys,
        values,
        residual,
        norm_gain.reshape(1, width),
        expert_ids,
        expert_gates,
        out_weight,
        w_gate,
        w_up,
        w_down,
    )
    return results[0], results[1]


def solution(mesh):
    one_block = mesh.shape["ctx"] == 2 and mesh.shape["exp"] == 16
    return jax.shard_map(
        layer_on_device if one_block else on_device,
        mesh=mesh,
        in_specs=(
            P("ctx", "exp"),
            P("ctx", None),
            P("ctx", None),
            P(("ctx", "exp"), None),
            P("exp", None),
            P(),
            P(("ctx", "exp"), None),
            P(("ctx", "exp"), None),
            P("exp", None, "ctx"),
            P("exp", None, "ctx"),
            P("exp", None, "ctx"),
        ),
        out_specs=(P(("ctx", "exp"), None), P(("ctx", "exp"), None)),
        check_vma=False,
    )
```
